32 devices in a mesh: rows: 8 (over z, y), band: 4 (over x, core).
Axes of the slice: x: 2, y: 2, z: 4, core: 2. Of those that a mesh axis runs over, the one named last changes fastest.
Arguments:
- frames: bfloat16 [2, 32, 512, 96], P(None, 'rows'), may hold values from -6 to 6
- conv_weight: bfloat16 [3, 3, 96, 128], replicated, may hold values from -0.21875 to 0.21875
- proj_weight: bfloat16 [128, 256], replicated, may hold values from -0.5 to 0.5
- band_start: int32 [8], P('rows'), may hold values from -4 to 4, as said below
- band_count: int32 [8], P('rows'), may hold values from 1 to 8, as said below
- pyramid_grad: bfloat16 [8, 2, 4, 512, 960], P('rows', None, 'band'), may hold values from -6 to 6
Outputs:
- pyramid: bfloat16 [8, 2, 4, 512, 960], P('rows', None, 'band')
- source_grad: float32 [16, 256, 256], P('rows', None, 'band')
- target_grad: float32 [16, 256, 256], P('rows', None, 'band')
The draws below stay inside these ranges and needn't reach their ends.
Inputs may be any that keep to these rules, and one draw needn't show every extreme that they name: Row block b's band covers target blocks b + band_start[b] to b + band_start[b] + band_count[b] - 1, all within b - 4 to b + 4. `band_count`: some row block's band has 8 target blocks and some other's has 1.
All inputs are finite; a program needn't handle non-finite values.
Results may differ from the reference program's by a relative error of at most 0.0034.
Values may be sent and summed in bfloat16 or wider, within the bound.
No kernel may reach another device: no remote copies, remote signals or barrier semaphores. Data moves between devices by JAX's collectives and lax.ppermute only.
A program may use at most 128 MiB of HBM per device.

```python
import math
import jax
import jax.numpy as jnp
from jax import lax

IN_CHANNELS = 96
MID_CHANNELS = 128
CHANNELS = 256
LEVELS = 4
ROWS_DEV = 2
COLUMNS = 256
BAND_REACH = 4
SLOTS_DEV = 2
FEAT_ROWS = 16
PIXELS = 512
PYRAMID = 960
SLOTS = 8
N_ROWS = 8
N_BAND = 4


def band_tables(key):
    base = jax.random.fold_in(key, 7)
    keys = jax.random.split(base, 6)
    wide = jax.random.randint(keys[0], (N_ROWS,), 0, 4) == 0
    narrow_count = jax.random.randint(keys[1], (N_ROWS,), 1, SLOTS // 2)
    wide_count = jax.random.randint(keys[2], (N_ROWS,), SLOTS // 2 + 1, SLOTS + 1)
    counts = jnp.where(wide, wide_count, narrow_count)
    last = N_ROWS - 1
    before = N_ROWS - 2
    second = jax.random.randint(keys[4], (), 0, N_ROWS - 2)
    places = jnp.arange(N_ROWS, dtype=jnp.int32)
    counts = jnp.where(places == last, SLOTS, counts)
    counts = jnp.where(places == before, N_BAND, counts)
    counts = jnp.where(places == second, 1, counts)
    starts = jax.random.randint(keys[5], (N_ROWS,), -BAND_REACH, BAND_REACH + 2 - counts)
    starts = jnp.where(places == last, -BAND_REACH, starts)
    starts = jnp.where(places == before, 2 - N_BAND, starts)
    starts = jnp.where(places == second, BAND_REACH, starts)
    return (starts.astype(jnp.int32), counts.astype(jnp.int32))


def draw_band_start(key, part):
    return band_tables(key)[0]


def draw_band_count(key, part):
    return band_tables(key)[1]


def block_scale(stream_key, extent, cuts, low, top_value):
    def one(axis_at, shards_of):
        heights = jax.random.uniform(jax.random.fold_in(jax.random.fold_in(stream_key, 6), axis_at), (shards_of,), jnp.float32, low / len(cuts), top_value / len(cuts))
        return jnp.repeat(jnp.exp(heights), extent[axis_at] // shards_of).reshape((-1,) + (1,) * (len(extent) - axis_at - 1))

    factor_of = one(*cuts[0])
    for cut in cuts[1:]:
        factor_of = factor_of * one(*cut)
    return factor_of


def bell_draw(rng, shape, deviation, most, pieces=(), kind=jnp.bfloat16):
    array = deviation * jax.random.normal(rng, shape, jnp.float32)
    if pieces:
        array = array * block_scale(rng, shape, pieces, -0.22, 0.18)
    return jnp.clip(array, -most, most).astype(kind)


def setup_inputs(seed: int = 0) -> dict:
    key_of = jax.random.split(jax.random.key(seed), 7)
    return {
        "frames": bell_draw(key_of[0], (2, 2 * FEAT_ROWS, 2 * COLUMNS, IN_CHANNELS), 1.0, 6.0, ((1, 8),)),
        "conv_weight": bell_draw(key_of[1], (3, 3, IN_CHANNELS, MID_CHANNELS), (9 * IN_CHANNELS) ** -0.5, 0.21875),
        "proj_weight": bell_draw(key_of[2], (MID_CHANNELS, CHANNELS), MID_CHANNELS ** -0.5, 0.5),
        "band_start": draw_band_start(jax.random.fold_in(key_of[6], 71), 0),
        "band_count": draw_band_count(jax.random.fold_in(key_of[6], 71), 0),
        "pyramid_grad": bell_draw(key_of[5], (N_ROWS, SLOTS_DEV, N_BAND, PIXELS, PYRAMID), 1.0, 6.0, ((0, 8), (2, 4))),
    }


def encode(frames, conv_weight, proj_weight):
    convolved = lax.conv_general_dilated(frames, conv_weight, (2, 2), ((1, 0), (1, 0)), dimension_numbers=('NHWC', 'HWIO', 'NHWC'), preferred_element_type=jnp.float32)
    middle = jax.nn.relu(convolved).astype(jnp.bfloat16)
    flattened = jnp.dot(middle.reshape(-1, MID_CHANNELS), proj_weight, preferred_element_type=jnp.float32)
    return flattened.reshape(2, N_ROWS, PIXELS, CHANNELS)

def pool_levels(correlation):
    row_count = correlation.shape[0]
    levels = []
    for level_index in range(LEVELS):
        group_size = 2 ** level_index
        pooled = correlation.reshape(row_count, ROWS_DEV, COLUMNS // group_size, group_size)
        levels.append(lax.optimization_barrier(jnp.mean(pooled, axis=3)).reshape(row_count, PIXELS // group_size))
    return jnp.concatenate(levels, axis=1)

def spread_levels(gradient):
    row_count = gradient.shape[0]
    summed = gradient[:, :PIXELS]
    column_start = PIXELS
    for level_index in range(1, LEVELS):
        group_size = 2 ** level_index
        level_width = PIXELS // group_size
        level_part = gradient[:, column_start:column_start + level_width].reshape(row_count, ROWS_DEV, level_width // ROWS_DEV, 1)
        spread = jnp.broadcast_to(level_part / group_size, (row_count, ROWS_DEV, level_width // ROWS_DEV, group_size))
        summed = summed + spread.reshape(row_count, PIXELS)
        column_start = column_start + level_width
    return summed

def reference(frames, conv_weight, proj_weight, band_start, band_count, pyramid_grad):
    features = encode(frames, conv_weight, proj_weight)
    margin = jnp.zeros((BAND_REACH, PIXELS, CHANNELS), jnp.float32)
    targets = jnp.concatenate([margin, features[1], margin], axis=0)
    factor = 1.0 / math.sqrt(CHANNELS)
    indices = jnp.arange(N_ROWS, dtype=jnp.int32)
    flat_grad = pyramid_grad.reshape(N_ROWS, SLOTS, PIXELS, PYRAMID)

    def one_block(carried, scanned):
        block_index, band_first, count_here, source, gradients = scanned
        pyramids = []
        source_sum = jnp.zeros((PIXELS, CHANNELS), jnp.float32)
        for slot_index in range(SLOTS):
            weight_on = (slot_index < count_here).astype(jnp.float32)
            window_place = (block_index + band_first + slot_index + BAND_REACH).astype(jnp.int32)
            target = lax.dynamic_index_in_dim(targets, window_place, 0, keepdims=False)
            correlation = jnp.dot(source, target.T, precision=lax.Precision.HIGHEST) * factor * weight_on
            pyramids.append(pool_levels(correlation).astype(jnp.bfloat16))
            grad_corr = spread_levels(gradients[slot_index].astype(jnp.float32)) * weight_on
            source_sum = source_sum + jnp.dot(grad_corr, target, precision=lax.Precision.HIGHEST) * factor
            target_part = jnp.dot(grad_corr.T, source, precision=lax.Precision.HIGHEST) * factor
            current = lax.dynamic_index_in_dim(carried, window_place, 0, keepdims=False)
            carried = lax.dynamic_update_index_in_dim(carried, current + target_part, window_place, 0)
        return (carried, (jnp.stack(pyramids), source_sum))
    initial = jnp.zeros((N_ROWS + 2 * BAND_REACH, PIXELS, CHANNELS), jnp.float32)
    carried, outputs = lax.scan(one_block, initial, (indices, band_start, band_count, features[0], flat_grad))
    pyramid, source_grad = outputs
    target_grad = carried[BAND_REACH:BAND_REACH + N_ROWS]
    pyramid = pyramid.reshape(N_ROWS, SLOTS_DEV, N_BAND, PIXELS, PYRAMID)
    return (pyramid, source_grad.reshape(FEAT_ROWS, COLUMNS, CHANNELS), target_grad.reshape(FEAT_ROWS, COLUMNS, CHANNELS))
```

```python
import math

import jax
import jax.numpy as jnp
import numpy as np
from jax import lax
from jax.experimental import pallas as pl
from jax.experimental.pallas import tpu as pltpu
from jax.sharding import PartitionSpec as P

LEVELS = 4
BAND_REACH = 4
F32 = jnp.float32
BF16 = jnp.bfloat16
VMEM_LIMIT = 56 * 1024 * 1024
NN = (((1,), (0,)), ((), ()))
NT = (((1,), (1,)), ((), ()))


def product(a, b, dims=NN):
    return lax.dot_general(a, b, dims, preferred_element_type=F32)


def halves(x):
    high = x.astype(BF16)
    return high, (x - high.astype(F32)).astype(BF16)


def spread_matrix(pixels):
    parts = []
    for level in range(LEVELS):
        group = 2**level
        parts.append(np.repeat(np.eye(pixels // group, dtype=np.float32), group, axis=0) / group)
    return np.concatenate(parts, axis=1).astype(jnp.bfloat16)


def convolve_row(rows, weight_ref, scratch):
    columns = rows[0].shape[0]
    mid = weight_ref.shape[3]
    total = None
    for dy in range(3):
        weight = jnp.concatenate([weight_ref[dy, dx] for dx in range(3)], axis=1)
        part = product(rows[dy], weight)
        total = part if total is None else total + part
    for dx in range(3):
        scratch[dx][8 : 8 + columns, :] = total[:, dx * mid : (dx + 1) * mid]
    out = sum(scratch[dx][pl.ds(7 + dx, columns // 2, stride=2), :] for dx in range(3))
    return jnp.maximum(out, 0.0)


def lower_rows_kernel(frames_ref, weight_ref, mid_ref, *scratch):
    scratch[0][0:8, :] = jnp.zeros((8, scratch[0].shape[1]), F32)
    for frame in range(2):
        rows = [frames_ref[frame, 1 + dy] for dy in range(3)]
        mid_ref[frame] = convolve_row(rows, weight_ref, scratch).astype(BF16)


def upper_rows_kernel(frames_ref, rim_ref, weight_ref, lower_ref, source_ref, source_t_ref, target_t_ref, *scratch):
    scratch[0][0:8, :] = jnp.zeros((8, scratch[0].shape[1]), F32)
    half = lower_ref.shape[1]
    for frame in range(2):
        rows = [rim_ref[frame, 0], frames_ref[frame, 0], frames_ref[frame, 1]]
        upper = convolve_row(rows, weight_ref, scratch)
        lower = lower_ref[frame]
        out_t = source_t_ref if frame == 0 else target_t_ref
        out_t[:, :half] = upper.T.astype(BF16)
        out_t[:, half:] = lower.astype(F32).T.astype(BF16)
        if frame == 0:
            source_ref[:half, :] = upper.astype(BF16)
            source_ref[half:, :] = lower


def encode(frames, rim, conv_weight):
    _, rows, columns, _ = frames.shape
    mid = conv_weight.shape[3]
    half = columns // 2
    scratch = [pltpu.VMEM((8 + columns + 8, mid), F32) for _ in range(3)]
    params = pltpu.CompilerParams(vmem_limit_bytes=VMEM_LIMIT)
    lower = pl.pallas_call(
        lower_rows_kernel,
        out_shape=jax.ShapeDtypeStruct((2, half, mid), BF16),
        scratch_shapes=scratch,
        compiler_params=params,
        cost_estimate=pl.CostEstimate(flops=2**29, bytes_accessed=2**20, transcendentals=0),
    )(frames, conv_weight)
    pixels = 2 * half
    return pl.pallas_call(
        upper_rows_kernel,
        out_shape=(
            jax.ShapeDtypeStruct((pixels, mid), BF16),
            jax.ShapeDtypeStruct((mid, pixels), BF16),
            jax.ShapeDtypeStruct((mid, pixels), BF16),
        ),
        scratch_shapes=scratch,
        compiler_params=params,
        cost_estimate=pl.CostEstimate(flops=2**29, bytes_accessed=2**20, transcendentals=0),
    )(frames, rim, conv_weight, lower)


def target_kernel(band, factor, count_ref, source_ref, source_t_ref, grad_ref, spread_ref, proj_ref, tile_ref, scaled_ref):
    slot = pl.program_id(0)
    active = slot * band + lax.axis_index("band") < count_ref[0]
    mid = source_ref.shape[1]

    @pl.when(slot == 0)
    def _():
        gram_high, gram_low = halves(product(proj_ref[...], proj_ref[...], NT))
        both = product(source_ref[...], jnp.concatenate([gram_high, gram_low], axis=1))
        high, low = halves((both[:, :mid] + both[:, mid:]) * factor)
        scaled_ref[:, :mid] = high
        scaled_ref[:, mid:] = low

    @pl.when(active)
    def _():
        high, low = halves(product(source_t_ref[...], grad_ref[0, 0, 0]))
        both = product(spread_ref[...], jnp.concatenate([high, low], axis=0), NT)
        tile_ref[0] = (both[:, :mid] + both[:, mid:]).astype(BF16)

    @pl.when(jnp.logical_not(active))
    def _():
        tile_ref[0] = jnp.zeros(tile_ref.shape[1:], BF16)


def pyramid_kernel(band, start_ref, count_ref, held_ref, other_ref, scaled_ref, grad_ref, spread_ref, pyramid_ref, sum_ref):
    slot = pl.program_id(0)
    active = slot * band + lax.axis_index("band") < count_ref[0]
    even = lax.rem(start_ref[0] + 2 * BAND_REACH, 2) == 0
    mid = held_ref.shape[1]

    @pl.when(slot == 0)
    def _():
        sum_ref[...] = jnp.zeros(sum_ref.shape, F32)

    @pl.when(active)
    def _():
        target = jnp.where(even, held_ref[0], other_ref[0])
        high, low = halves(product(target, spread_ref[...]))
        corr = product(scaled_ref[...], jnp.concatenate([high, high], axis=0))
        corr = corr + product(scaled_ref[:, :mid], low)
        pyramid_ref[0, 0, 0] = corr.astype(BF16)
        both = product(grad_ref[0, 0, 0], jnp.concatenate([high, low], axis=0), NT)
        sum_ref[...] += both[:, :mid] + both[:, mid:]

    @pl.when(jnp.logical_not(active))
    def _():
        pyramid_ref[0, 0, 0] = jnp.zeros(pyramid_ref.shape[3:], BF16)


def project_kernel(factor, sum_ref, own_ref, *refs):
    band = refs[-1].shape[0] + 1
    parts, weight_ref, kept_ref, sent_ref = refs[:-3], refs[-3], refs[-2], refs[-1]
    place = lax.axis_index("band")
    target = own_ref[...].astype(F32)
    for part in parts:
        target = target + part[...].astype(F32)
    high, low = halves(jnp.concatenate([sum_ref[...], target], axis=1))
    for k in range(band):
        weight = weight_ref[jnp.bitwise_xor(place, k)]
        out = (product(high, weight) + product(low, weight)) * factor
        if k == 0:
            kept_ref[...] = out
        else:
            sent_ref[k - 1] = out.astype(BF16)


def shards(frames, conv_weight, proj_weight, band_start, band_count, pyramid_grad):
    band = lax.axis_size("band")
    row_blocks = lax.axis_size("rows")
    place = lax.axis_index("band")
    channels = proj_weight.shape[1]
    mid = proj_weight.shape[0]
    share = channels // band
    factor = 1.0 / math.sqrt(channels)
    slots = pyramid_grad.shape[1]
    pixels, entries = pyramid_grad.shape[3:]
    columns = frames.shape[2] // 2
    params = pltpu.CompilerParams(vmem_limit_bytes=VMEM_LIMIT)
    smem = pl.BlockSpec(memory_space=pltpu.SMEM)
    spread = jnp.asarray(spread_matrix(pixels))

    offsets = ([], [])
    for reach in range(1, BAND_REACH + 1):
        offsets[reach % 2].extend([reach, -reach])

    def along_rows(x, step, sign):
        pairs = []
        for row in range(row_blocks):
            for p in range(band):
                to = row + sign * offsets[p % 2][step]
                if 0 <= to < row_blocks:
                    pairs.append((row * band + p, to * band + p))
        return lax.ppermute(x, ("rows", "band"), pairs)

    def across(x, k):
        return lax.ppermute(x, "band", [(p, p ^ k) for p in range(band)])

    parity = place % 2
    step_offsets = [jnp.where(parity == 0, offsets[0][i], offsets[1][i]) for i in range(len(offsets[0]))]
    start = band_start[0]
    swap = start % 2
    held_offsets = [start + j * band + (place - parity) + (parity + swap) % 2 for j in range(slots)]

    rim = lax.ppermute(frames[:, -1:], "rows", [(i, i + 1) for i in range(row_blocks - 1)])
    source, source_t, target_t = encode(frames, rim, conv_weight)

    arrived = [along_rows(target_t, i, -1) for i in range(len(step_offsets))]

    grad_spec = pl.BlockSpec((1, 1, 1, pixels, entries), lambda j: (0, j, 0, 0, 0))

    def whole(shape):
        return pl.BlockSpec(shape, lambda j: (0,) * len(shape))

    tiles, scaled = pl.pallas_call(
        lambda *refs: target_kernel(band, factor, *refs),
        grid=(slots,),
        in_specs=[smem, whole((pixels, mid)), whole((mid, pixels)), grad_spec, whole((pixels, entries)), whole((mid, channels))],
        out_specs=(pl.BlockSpec((1, pixels, mid), lambda j: (j, 0, 0)), whole((pixels, 2 * mid))),
        out_shape=(
            jax.ShapeDtypeStruct((slots, pixels, mid), BF16),
            jax.ShapeDtypeStruct((pixels, 2 * mid), BF16),
        ),
        compiler_params=params,
        cost_estimate=pl.CostEstimate(flops=2**30, bytes_accessed=2**22, transcendentals=0),
    )(band_count, source, source_t, pyramid_grad, spread, proj_weight)

    other_tiles = across(tiles, 1)
    moved = [jnp.where(swap == 0, tiles[j], other_tiles[j]) for j in range(slots)]

    def term(offset):
        out = jnp.zeros((pixels, mid), BF16)
        for j in range(slots):
            out = jnp.where(held_offsets[j] == offset, moved[j], out)
        return out

    own_term = term(0)
    received = [along_rows(term(step_offsets[i]), i, 1) for i in range(len(step_offsets))]

    def pick(offset):
        out = target_t
        for i in range(len(step_offsets)):
            out = jnp.where(offset == step_offsets[i], arrived[i], out)
        return out

    held = jnp.stack([pick(offset) for offset in held_offsets])
    other = across(held, 1)

    target_spec = pl.BlockSpec((1, mid, pixels), lambda j: (j, 0, 0))
    pyramid, source_sum = pl.pallas_call(
        lambda *refs: pyramid_kernel(band, *refs),
        grid=(slots,),
        in_specs=[smem, smem, target_spec, target_spec, whole((pixels, 2 * mid)), grad_spec, whole((pixels, entries))],
        out_specs=(grad_spec, whole((pixels, mid))),
        out_shape=(
            jax.ShapeDtypeStruct(pyramid_grad.shape, BF16),
            jax.ShapeDtypeStruct((pixels, mid), F32),
        ),
        compiler_params=params,
        cost_estimate=pl.CostEstimate(flops=2**31, bytes_accessed=2**22, transcendentals=0),
    )(band_start, band_count, held, other, scaled, pyramid_grad, spread)

    empty = jnp.zeros((mid, share), BF16)
    weights = jnp.stack(
        [
            jnp.block([[proj_weight[:, q * share : (q + 1) * share], empty], [empty, proj_weight[:, q * share : (q + 1) * share]]])
            for q in range(band)
        ]
    )
    kept, sent = pl.pallas_call(
        lambda *refs: project_kernel(factor, *refs),
        out_shape=(
            jax.ShapeDtypeStruct((pixels, 2 * share), F32),
            jax.ShapeDtypeStruct((band - 1, pixels, 2 * share), BF16),
        ),
        compiler_params=params,
        cost_estimate=pl.CostEstimate(flops=2**29, bytes_accessed=2**21, transcendentals=0),
    )(source_sum, own_term, *received, weights)
    total = kept
    for k in range(1, band):
        total = total + across(sent[k - 1], k).astype(F32)
    shape_out = (pixels // columns, columns, share)
    return (pyramid, total[:, :share].reshape(shape_out), total[:, share:].reshape(shape_out))


def solution(mesh):
    in_specs = (
        P(None, "rows", None, None),
        P(),
        P(),
        P("rows"),
        P("rows"),
        P("rows", None, "band", None, None),
    )
    out_specs = (
        P("rows", None, "band", None, None),
        P("rows", None, "band"),
        P("rows", None, "band"),
    )
    return jax.shard_map(shards, mesh=mesh, in_specs=in_specs, out_specs=out_specs, check_vma=False)
```

```python
import math

import jax
import jax.numpy as jnp
import numpy as np
from jax import lax
from jax.experimental import pallas as pl
from jax.experimental.pallas import tpu as pltpu
from jax.sharding import PartitionSpec as P

LEVELS = 4
BAND_REACH = 4
F32 = jnp.float32
BF16 = jnp.bfloat16
VMEM_LIMIT = 28 * 1024 * 1024
NN = (((1,), (0,)), ((), ()))
NT = (((1,), (1,)), ((), ()))
TN = (((0,), (0,)), ((), ()))


def product(a, b, dims=NN):
    return lax.dot_general(a, b, dims, preferred_element_type=F32)


def halves(x):
    high = x.astype(BF16)
    return high, (x - high.astype(F32)).astype(BF16)


def spread_matrix(pixels):
    parts = []
    for level in range(LEVELS):
        group = 2**level
        parts.append(np.repeat(np.eye(pixels // group, dtype=np.float32), group, axis=1) / group)
    return np.concatenate(parts, axis=0).astype(jnp.bfloat16)


def column_picker(columns):
    half = columns // 2
    taps = [
        (
            lax.broadcasted_iota(jnp.int32, (columns, half), 0)
            == 2 * lax.broadcasted_iota(jnp.int32, (columns, half), 1) + (dx - 1)
        )
        for dx in range(3)
    ]
    return jnp.concatenate([jnp.where(tap, 1.0, 0.0).astype(BF16) for tap in taps], axis=1)


def gathered(picked, rows, half):
    return jnp.concatenate(
        [
            jnp.concatenate([picked(frame, row)[:, dx * half : (dx + 1) * half] for frame in range(2)], axis=1)
            for row in rows
            for dx in range(3)
        ],
        axis=0,
    )


def stacked_weight(weight_ref, taps):
    return jnp.concatenate([weight_ref[dy, dx] for dy in taps for dx in range(3)], axis=0)


def local_rows_kernel(frames_ref, weight_ref, proj_ref, lower_ref, partial_ref, picker_ref, gram_ref, pick_ref):
    _, rows, channels, columns = frames_ref.shape
    half = columns // 2
    mid = weight_ref.shape[3]
    picker_ref[...] = column_picker(columns)
    flat = frames_ref[...].reshape(2 * rows * channels, columns)
    pick_ref[...] = product(flat, picker_ref[...]).astype(BF16).reshape(pick_ref.shape)

    def picked(frame, row):
        return pick_ref[frame, row]

    lower = product(stacked_weight(weight_ref, range(3)), gathered(picked, (1, 2, 3), half), TN)
    lower_ref[...] = jnp.maximum(lower, 0.0).astype(BF16)
    partial_ref[...] = product(stacked_weight(weight_ref, (1, 2)), gathered(picked, (0, 1), half), TN)
    gram_high, gram_low = halves(product(proj_ref[...], proj_ref[...], NT))
    gram_ref[:mid, :] = gram_high
    gram_ref[mid:, :] = gram_low


def target_kernel(
    band, factor, count_ref, rim_ref, weight_ref, lower_ref, partial_ref, picker_ref, gram_ref, grad_ref, spread_ref,
    target_ref, tile_ref, scaled_ref
):
    half = lower_ref.shape[1] // 2
    mid = lower_ref.shape[0]
    channels = rim_ref.shape[2]
    pick = product(rim_ref[...].reshape(2 * channels, 2 * half), picker_ref[...]).astype(BF16)

    def picked(frame, row):
        return pick[frame * channels : (frame + 1) * channels]

    upper = product(stacked_weight(weight_ref, (0,)), gathered(picked, (0,), half), TN) + partial_ref[...]
    upper = jnp.maximum(upper, 0.0).astype(BF16)
    source = jnp.concatenate([upper[:, :half], lower_ref[:, :half]], axis=1)
    target_ref[:, :half] = upper[:, half:]
    target_ref[:, half:] = lower_ref[:, half:]
    both = product(gram_ref[...], source)
    high, low = halves((both[:mid] + both[mid:]) * factor)
    scaled_ref[:mid, :] = high
    scaled_ref[mid : 2 * mid, :] = low
    scaled_ref[2 * mid :, :] = high
    for slot in range(tile_ref.shape[0]):
        active = slot * band + lax.axis_index("band") < count_ref[0]

        @pl.when(active)
        def _():
            high, low = halves(product(source, grad_ref[0, slot, 0], NT))
            both = product(jnp.concatenate([high, low], axis=0), spread_ref[...])
            tile_ref[slot] = (both[:mid] + both[mid:]).astype(BF16)

        @pl.when(jnp.logical_not(active))
        def _():
            tile_ref[slot] = jnp.zeros(tile_ref.shape[1:], BF16)


def pyramid_kernel(
    band, factor, start_ref, count_ref, held_ref, other_ref, scaled_ref, grad_ref, spread_ref, proj_ref, own_ref, *refs
):
    parts, (pyramid_ref, kept_ref, sent_ref, sum_ref, out_ref) = refs[:-5], refs[-5:]
    slot = pl.program_id(0)
    place = lax.axis_index("band")
    active = slot * band + place < count_ref[0]
    even = lax.rem(start_ref[0] + 2 * BAND_REACH, 2) == 0
    mid, pixels = held_ref.shape[1:]

    @pl.when(slot == 0)
    def _():
        sum_ref[...] = jnp.zeros(sum_ref.shape, F32)

    @pl.when(active)
    def _():
        target = jnp.where(even, held_ref[0], other_ref[0])
        high, low = halves(product(spread_ref[...], target, NT))
        corr = product(jnp.concatenate([high, high, low], axis=1), scaled_ref[...])
        pyramid_ref[0, 0, 0] = corr.astype(BF16)
        high, low = halves(product(target, spread_ref[...], NT))
        both = product(jnp.concatenate([high, low], axis=0), grad_ref[0, 0, 0])
        sum_ref[...] += both[:mid] + both[mid:]

    @pl.when(jnp.logical_not(active))
    def _():
        pyramid_ref[0, 0, 0] = jnp.zeros(pyramid_ref.shape[3:], BF16)

    @pl.when(slot == pl.num_programs(0) - 1)
    def _():
        target = own_ref[...].astype(F32)
        for part in parts:
            target = target + part[1].astype(F32)
        high, low = halves(jnp.concatenate([sum_ref[...], target], axis=1))
        out_ref[...] = (product(proj_ref[...], high, TN) + product(proj_ref[...], low, TN)) * factor
        share, width = kept_ref.shape[1:]
        for k in range(band):
            first = pl.multiple_of(jnp.bitwise_xor(place, k) * share, share)
            for part in range(kept_ref.shape[0]):
                out = out_ref[pl.ds(first, share), part * width : (part + 1) * width]
                if k == 0:
                    kept_ref[part] = out
                else:
                    sent_ref[k - 1, part] = out.astype(BF16)


def shards(frames, conv_weight, proj_weight, band_start, band_count, pyramid_grad):
    band = lax.axis_size("band")
    row_blocks = lax.axis_size("rows")
    place = lax.axis_index("band")
    mid, channels = proj_weight.shape
    share = channels // band
    factor = 1.0 / math.sqrt(channels)
    frames = jnp.swapaxes(frames, 2, 3)
    grad = jnp.swapaxes(pyramid_grad, 3, 4)
    slots = grad.shape[1]
    entries, pixels = grad.shape[3:]
    columns = frames.shape[3]
    half = columns // 2
    params = pltpu.CompilerParams(vmem_limit_bytes=VMEM_LIMIT)
    smem = pl.BlockSpec(memory_space=pltpu.SMEM)
    vmem = pl.BlockSpec(memory_space=pltpu.VMEM)
    spread = jnp.asarray(spread_matrix(pixels))

    offsets = ([], [])
    for reach in range(1, BAND_REACH + 1):
        offsets[reach % 2].extend([reach, -reach])

    def along_rows(x, step):
        pairs = []
        for row in range(row_blocks):
            for p in range(band):
                to = row - offsets[p % 2][step]
                if 0 <= to < row_blocks:
                    pairs.append((row * band + p, to * band + p))
        return lax.ppermute(x, ("rows", "band"), pairs)

    def across(x, k):
        return lax.ppermute(x, "band", [(p, p ^ k) for p in range(band)])

    parity = place % 2
    step_offsets = [jnp.where(parity == 0, offsets[0][i], offsets[1][i]) for i in range(len(offsets[0]))]
    start = band_start[0]
    swap = start % 2
    held_offsets = [start + j * band + (place - parity) + (parity + swap) % 2 for j in range(slots)]

    rim = lax.ppermute(frames[:, -1:], "rows", [(i, i + 1) for i in range(row_blocks - 1)])
    lower, partial, picker, gram = pl.pallas_call(
        local_rows_kernel,
        out_shape=(
            jax.ShapeDtypeStruct((mid, columns), BF16),
            jax.ShapeDtypeStruct((mid, columns), F32),
            jax.ShapeDtypeStruct((columns, 3 * half), BF16),
            jax.ShapeDtypeStruct((2 * mid, mid), BF16),
        ),
        scratch_shapes=[pltpu.VMEM(frames.shape[:3] + (3 * half,), BF16)],
        compiler_params=params,
        cost_estimate=pl.CostEstimate(flops=2**31, bytes_accessed=2**21, transcendentals=0),
    )(frames, conv_weight, proj_weight)

    target, tiles, scaled = pl.pallas_call(
        lambda *refs: target_kernel(band, factor, *refs),
        in_specs=[smem] + [vmem] * 8,
        out_shape=(
            jax.ShapeDtypeStruct((mid, pixels), BF16),
            jax.ShapeDtypeStruct((slots, mid, pixels), BF16),
            jax.ShapeDtypeStruct((3 * mid, pixels), BF16),
        ),
        compiler_params=params,
        cost_estimate=pl.CostEstimate(flops=2**31, bytes_accessed=2**22, transcendentals=0),
    )(band_count, rim, conv_weight, lower, partial, picker, gram, grad, spread)

    other_tiles = across(tiles, 1)
    moved = [jnp.where(swap == 0, tiles[j], other_tiles[j]) for j in range(slots)]

    def term(offset):
        out = jnp.zeros((mid, pixels), BF16)
        for j in range(slots):
            out = jnp.where(held_offsets[j] == offset, moved[j], out)
        return out

    own_term = term(0)
    arrived = [
        along_rows(jnp.stack([target, term(-step_offsets[i])]), i) for i in range(len(step_offsets))
    ]

    def pick(offset):
        out = target
        for i in range(len(step_offsets)):
            out = jnp.where(offset == step_offsets[i], arrived[i][0], out)
        return out

    held = jnp.stack([pick(offset) for offset in held_offsets])
    other = across(held, 1)

    def whole(shape):
        return pl.BlockSpec(shape, lambda j: (0,) * len(shape))

    target_spec = pl.BlockSpec((1, mid, pixels), lambda j: (j, 0, 0))
    grad_spec = pl.BlockSpec((1, 1, 1, entries, pixels), lambda j: (0, j, 0, 0, 0))
    out_parts = 2 * pixels // half
    pyramid, kept, sent = pl.pallas_call(
        lambda *refs: pyramid_kernel(band, factor, *refs),
        grid=(slots,),
        in_specs=[smem, smem, target_spec, target_spec, whole((3 * mid, pixels)), grad_spec, whole((entries, pixels))]
        + [whole((mid, channels)), whole((mid, pixels))]
        + [whole((2, mid, pixels)) for _ in arrived],
        out_specs=(grad_spec, whole((out_parts, share, half)), whole((band - 1, out_parts, share, half))),
        out_shape=(
            jax.ShapeDtypeStruct(grad.shape, BF16),
            jax.ShapeDtypeStruct((out_parts, share, half), F32),
            jax.ShapeDtypeStruct((band - 1, out_parts, share, half), BF16),
        ),
        scratch_shapes=[pltpu.VMEM((mid, pixels), F32), pltpu.VMEM((channels, 2 * pixels), F32)],
        compiler_params=params,
        cost_estimate=pl.CostEstimate(flops=2**31, bytes_accessed=2**22, transcendentals=0),
    )(band_start, band_count, held, other, scaled, grad, spread, proj_weight, own_term, *arrived)

    total = kept
    for k in range(1, band):
        total = total + across(sent[k - 1], k).astype(F32)
    total = jnp.swapaxes(total, 1, 2)
    return (jnp.swapaxes(pyramid, 3, 4), total[: out_parts // 2], total[out_parts // 2 :])


def solution(mesh):
    in_specs = (
        P(None, "rows", None, None),
        P(),
        P(),
        P("rows"),
        P("rows"),
        P("rows", None, "band", None, None),
    )
    out_specs = (
        P("rows", None, "band", None, None),
        P("rows", None, "band"),
        P("rows", None, "band"),
    )
    return jax.shard_map(shards, mesh=mesh, in_specs=in_specs, out_specs=out_specs, check_vma=False)
```

```python
import math

import jax
import jax.numpy as jnp
import numpy as np
from jax import lax
from jax.experimental import pallas as pl
from jax.experimental.pallas import tpu as pltpu
from jax.sharding import PartitionSpec as P

LEVELS = 4
BAND_REACH = 4
F32 = jnp.float32
BF16 = jnp.bfloat16
VMEM_LIMIT = 28 * 1024 * 1024
NN = (((1,), (0,)), ((), ()))
NT = (((1,), (1,)), ((), ()))
TN = (((0,), (0,)), ((), ()))


def product(a, b, dims=NN):
    return lax.dot_general(a, b, dims, preferred_element_type=F32)


def halves(x):
    high = x.astype(BF16)
    return high, (x - high.astype(F32)).astype(BF16)


def spread_matrix(pixels):
    parts = []
    for level in range(LEVELS):
        group = 2**level
        parts.append(np.repeat(np.eye(pixels // group, dtype=np.float32), group, axis=1) / group)
    return np.concatenate(parts, axis=0).astype(jnp.bfloat16)


def column_picker(columns):
    half = columns // 2
    taps = [
        (
            lax.broadcasted_iota(jnp.int32, (columns, half), 0)
            == 2 * lax.broadcasted_iota(jnp.int32, (columns, half), 1) + (dx - 1)
        )
        for dx in range(3)
    ]
    return jnp.concatenate([jnp.where(tap, 1.0, 0.0).astype(BF16) for tap in taps], axis=1)


def gathered(picked, rows, half):
    return jnp.concatenate(
        [
            jnp.concatenate([picked(frame, row)[:, dx * half : (dx + 1) * half] for frame in range(2)], axis=1)
            for row in rows
            for dx in range(3)
        ],
        axis=0,
    )


def stacked_weight(weight_ref, taps):
    return jnp.concatenate([weight_ref[dy, dx] for dy in taps for dx in range(3)], axis=0)


def local_rows_kernel(frames_ref, weight_ref, proj_ref, lower_ref, partial_ref, picker_ref, gram_ref, pick_ref):
    _, rows, channels, columns = frames_ref.shape
    half = columns // 2
    mid = weight_ref.shape[3]
    picker_ref[...] = column_picker(columns)
    flat = frames_ref[...].reshape(2 * rows * channels, columns)
    pick_ref[...] = product(flat, picker_ref[...]).astype(BF16).reshape(pick_ref.shape)

    def picked(frame, row):
        return pick_ref[frame, row]

    lower = product(stacked_weight(weight_ref, range(3)), gathered(picked, (1, 2, 3), half), TN)
    lower_ref[...] = jnp.maximum(lower, 0.0).astype(BF16)
    partial_ref[...] = product(stacked_weight(weight_ref, (1, 2)), gathered(picked, (0, 1), half), TN)
    gram_high, gram_low = halves(product(proj_ref[...], proj_ref[...], NT))
    gram_ref[:mid, :] = gram_high
    gram_ref[mid:, :] = gram_low


def held_class(band, start_ref, count_ref, offsets, slots):
    place = lax.axis_index("band")
    core = lax.rem(place, 2)
    start = start_ref[0]
    swap = lax.rem(start + 2 * BAND_REACH, 2)
    slot_of = [j * band + place - core + lax.rem(core + swap, 2) for j in range(slots)]
    steps = [jnp.where(core == 0, even, odd) for even, odd in zip(*offsets)]
    return swap == 0, [start + k for k in slot_of], [k < count_ref[0] for k in slot_of], steps


def target_kernel(
    band, offsets, factor, start_ref, count_ref, rim_ref, weight_ref, lower_ref, partial_ref, picker_ref, gram_ref,
    grad_ref, other_ref, spread_ref, target_ref, scaled_ref, own_ref, *refs
):
    message_refs, tile_ref = refs[:-1], refs[-1]
    half = lower_ref.shape[1] // 2
    mid = lower_ref.shape[0]
    channels = rim_ref.shape[2]
    slots = tile_ref.shape[0]
    pick = product(rim_ref[...].reshape(2 * channels, 2 * half), picker_ref[...]).astype(BF16)

    def picked(frame, row):
        return pick[frame * channels : (frame + 1) * channels]

    upper = product(stacked_weight(weight_ref, (0,)), gathered(picked, (0,), half), TN) + partial_ref[...]
    upper = jnp.maximum(upper, 0.0).astype(BF16)
    source = jnp.concatenate([upper[:, :half], lower_ref[:, :half]], axis=1)
    target = jnp.concatenate([upper[:, half:], lower_ref[:, half:]], axis=1)
    both = product(gram_ref[...], source)
    high, low = halves((both[:mid] + both[mid:]) * factor)
    scaled_ref[:mid, :] = high
    scaled_ref[mid : 2 * mid, :] = low
    scaled_ref[2 * mid :, :] = high
    same, held, active, steps = held_class(band, start_ref, count_ref, offsets, slots)

    def term(slot, block_ref):
        high, low = halves(product(source, block_ref[0, slot, 0], NT))
        both = product(jnp.concatenate([high, low], axis=0), spread_ref[...])
        tile_ref[slot] = (both[:mid] + both[mid:]).astype(BF16)

    for slot in range(slots):
        pl.when(jnp.logical_and(active[slot], same))(lambda: term(slot, grad_ref))
        pl.when(jnp.logical_and(active[slot], jnp.logical_not(same)))(lambda: term(slot, other_ref))

    def chosen(offset):
        out = jnp.zeros(tile_ref.shape[1:], BF16)
        for slot in range(slots):
            out = jnp.where(jnp.logical_and(active[slot], held[slot] == offset), tile_ref[slot], out)
        return out

    target_ref[...] = target
    own_ref[...] = chosen(0)
    for step, message_ref in zip(steps, message_refs):
        message_ref[0] = target
        message_ref[1] = chosen(-step)


def gradient_kernel(
    band, offsets, factor, start_ref, count_ref, grad_ref, other_ref, spread_ref, proj_ref, target_ref, own_ref, *refs
):
    arrived, (held_ref, kept_ref, *sent_refs, sum_ref, out_ref) = refs[: len(offsets[0])], refs[len(offsets[0]) :]
    slots, mid, pixels = held_ref.shape
    same, held, active, steps = held_class(band, start_ref, count_ref, offsets, slots)
    sum_ref[...] = jnp.zeros(sum_ref.shape, F32)

    def add(slot, block_ref):
        high, low = halves(product(held_ref[slot], spread_ref[...], NT))
        both = product(jnp.concatenate([high, low], axis=0), block_ref[0, slot, 0])
        sum_ref[...] += both[:mid] + both[mid:]

    for slot in range(slots):
        block = target_ref[...]
        for step, part in zip(steps, arrived):
            block = jnp.where(held[slot] == step, part[0], block)
        held_ref[slot] = block
        pl.when(jnp.logical_and(active[slot], same))(lambda: add(slot, grad_ref))
        pl.when(jnp.logical_and(active[slot], jnp.logical_not(same)))(lambda: add(slot, other_ref))

    total = own_ref[...].astype(F32)
    for part in arrived:
        total = total + part[1].astype(F32)
    high, low = halves(jnp.concatenate([sum_ref[...], total], axis=1))
    out_ref[...] = (product(proj_ref[...], high, TN) + product(proj_ref[...], low, TN)) * factor
    parts, share, width = kept_ref.shape
    place = lax.axis_index("band")
    for k in range(band):
        first = pl.multiple_of(jnp.bitwise_xor(place, k) * share, share)
        for part in range(parts):
            out = out_ref[pl.ds(first, share), part * width : (part + 1) * width]
            if k == 0:
                kept_ref[part] = out
            else:
                sent_refs[k - 1][part] = out.astype(BF16)


def pyramid_kernel(band, start_ref, count_ref, held_ref, other_ref, scaled_ref, spread_ref, pyramid_ref):
    slot = pl.program_id(0)
    active = slot * band + lax.axis_index("band") < count_ref[0]
    same = lax.rem(start_ref[0] + 2 * BAND_REACH, 2) == 0

    @pl.when(active)
    def _():
        target = jnp.where(same, held_ref[0], other_ref[0])
        high, low = halves(product(spread_ref[...], target, NT))
        corr = product(jnp.concatenate([high, high, low], axis=1), scaled_ref[...])
        pyramid_ref[0, 0, 0] = corr.astype(BF16)

    @pl.when(jnp.logical_not(active))
    def _():
        pyramid_ref[0, 0, 0] = jnp.zeros(pyramid_ref.shape[3:], BF16)


def shards(frames, conv_weight, proj_weight, band_start, band_count, pyramid_grad):
    band = lax.axis_size("band")
    row_blocks = lax.axis_size("rows")
    mid, channels = proj_weight.shape
    share = channels // band
    factor = 1.0 / math.sqrt(channels)
    frames = jnp.swapaxes(frames, 2, 3)
    grad = jnp.swapaxes(pyramid_grad, 3, 4)
    slots = grad.shape[1]
    entries, pixels = grad.shape[3:]
    columns = frames.shape[3]
    half = columns // 2
    params = pltpu.CompilerParams(vmem_limit_bytes=VMEM_LIMIT)
    smem = pl.BlockSpec(memory_space=pltpu.SMEM)
    vmem = pl.BlockSpec(memory_space=pltpu.VMEM)
    spread = jnp.asarray(spread_matrix(pixels))

    offsets = ([], [])
    for reach in range(1, BAND_REACH + 1):
        offsets[reach % 2].extend([reach, -reach])
    steps = len(offsets[0])

    def along_rows(x, step):
        pairs = []
        for row in range(row_blocks):
            for p in range(band):
                to = row - offsets[p % 2][step]
                if 0 <= to < row_blocks:
                    pairs.append((row * band + p, to * band + p))
        return lax.ppermute(x, ("rows", "band"), pairs)

    def across(x, k):
        return lax.ppermute(x, "band", [(p, p ^ k) for p in range(band)])

    rim = lax.ppermute(frames[:, -1:], "rows", [(i, i + 1) for i in range(row_blocks - 1)])
    other_grad = across(grad, 1)
    lower, partial, picker, gram = pl.pallas_call(
        local_rows_kernel,
        out_shape=(
            jax.ShapeDtypeStruct((mid, columns), BF16),
            jax.ShapeDtypeStruct((mid, columns), F32),
            jax.ShapeDtypeStruct((columns, 3 * half), BF16),
            jax.ShapeDtypeStruct((2 * mid, mid), BF16),
        ),
        scratch_shapes=[pltpu.VMEM(frames.shape[:3] + (3 * half,), BF16)],
        compiler_params=params,
        cost_estimate=pl.CostEstimate(flops=2**31, bytes_accessed=2**21, transcendentals=0),
    )(frames, conv_weight, proj_weight)

    block = jax.ShapeDtypeStruct((mid, pixels), BF16)
    message = jax.ShapeDtypeStruct((2, mid, pixels), BF16)
    target, scaled, own_term, *messages = pl.pallas_call(
        lambda *refs: target_kernel(band, offsets, factor, *refs),
        in_specs=[smem] * 2 + [vmem] * 9,
        out_shape=(block, jax.ShapeDtypeStruct((3 * mid, pixels), BF16), block) + (message,) * steps,
        scratch_shapes=[pltpu.VMEM((slots, mid, pixels), BF16)],
        compiler_params=params,
        cost_estimate=pl.CostEstimate(flops=2**31, bytes_accessed=2**22, transcendentals=0),
    )(band_start, band_count, rim, conv_weight, lower, partial, picker, gram, grad, other_grad, spread)

    arrived = [along_rows(messages[i], i) for i in range(steps)]

    out_parts = 2 * pixels // half
    part = (out_parts, share, half)
    held, kept, *sent = pl.pallas_call(
        lambda *refs: gradient_kernel(band, offsets, factor, *refs),
        in_specs=[smem] * 2 + [vmem] * (6 + steps),
        out_shape=(jax.ShapeDtypeStruct((slots, mid, pixels), BF16), jax.ShapeDtypeStruct(part, F32))
        + (jax.ShapeDtypeStruct(part, BF16),) * (band - 1),
        scratch_shapes=[pltpu.VMEM((mid, pixels), F32), pltpu.VMEM((channels, 2 * pixels), F32)],
        compiler_params=params,
        cost_estimate=pl.CostEstimate(flops=2**31, bytes_accessed=2**22, transcendentals=0),
    )(band_start, band_count, grad, other_grad, spread, proj_weight, target, own_term, *arrived)

    received = [across(sent[k - 1], k) for k in reversed(range(1, band))]
    other = across(held, 1)

    def whole(shape):
        return pl.BlockSpec(shape, lambda j: (0,) * len(shape))

    target_spec = pl.BlockSpec((1, mid, pixels), lambda j: (j, 0, 0))
    grad_spec = pl.BlockSpec((1, 1, 1, entries, pixels), lambda j: (0, j, 0, 0, 0))
    pyramid = pl.pallas_call(
        lambda *refs: pyramid_kernel(band, *refs),
        grid=(slots,),
        in_specs=[smem, smem, target_spec, target_spec, whole((3 * mid, pixels)), whole((entries, pixels))],
        out_specs=grad_spec,
        out_shape=jax.ShapeDtypeStruct(grad.shape, BF16),
        compiler_params=params,
        cost_estimate=pl.CostEstimate(flops=2**31, bytes_accessed=2**22, transcendentals=0),
    )(band_start, band_count, held, other, scaled, spread)

    total, pyramid = lax.optimization_barrier((kept, pyramid))
    for x in received:
        total = total + x.astype(F32)
    total = jnp.swapaxes(total, 1, 2)
    return (jnp.swapaxes(pyramid, 3, 4), total[: out_parts // 2], total[out_parts // 2 :])


def solution(mesh):
    in_specs = (
        P(None, "rows", None, None),
        P(),
        P(),
        P("rows"),
        P("rows"),
        P("rows", None, "band", None, None),
    )
    out_specs = (
        P("rows", None, "band", None, None),
        P("rows", None, "band"),
        P("rows", None, "band"),
    )
    return jax.shard_map(shards, mesh=mesh, in_specs=in_specs, out_specs=out_specs, check_vma=False)
```

```python
import math

import jax
import jax.numpy as jnp
import numpy as np
from jax import lax
from jax.experimental import pallas as pl
from jax.experimental.pallas import tpu as pltpu
from jax.sharding import PartitionSpec as P

LEVELS = 4
BAND_REACH = 4
F32 = jnp.float32
BF16 = jnp.bfloat16
VMEM_LIMIT = 28 * 1024 * 1024
NN = (((1,), (0,)), ((), ()))
NT = (((1,), (1,)), ((), ()))
TN = (((0,), (0,)), ((), ()))


def product(a, b, dims=NN):
    return lax.dot_general(a, b, dims, preferred_element_type=F32)


def halves(x):
    high = x.astype(BF16)
    return high, (x - high.astype(F32)).astype(BF16)


def spread_matrix(pixels):
    parts = []
    for level in range(LEVELS):
        group = 2**level
        parts.append(np.repeat(np.eye(pixels // group, dtype=np.float32), group, axis=1) / group)
    return np.concatenate(parts, axis=0).astype(jnp.bfloat16)


def column_picker(columns):
    half = columns // 2
    taps = [
        (
            lax.broadcasted_iota(jnp.int32, (columns, half), 0)
            == 2 * lax.broadcasted_iota(jnp.int32, (columns, half), 1) + (dx - 1)
        )
        for dx in range(3)
    ]
    return jnp.concatenate([jnp.where(tap, 1.0, 0.0).astype(BF16) for tap in taps], axis=1)


def gathered(picked, rows, half):
    return jnp.concatenate(
        [
            jnp.concatenate([picked(frame, row)[:, dx * half : (dx + 1) * half] for frame in range(2)], axis=1)
            for row in rows
            for dx in range(3)
        ],
        axis=0,
    )


def stacked_weight(weight_ref, taps):
    return jnp.concatenate([weight_ref[dy, dx] for dy in taps for dx in range(3)], axis=0)


def local_rows_kernel(frames_ref, weight_ref, lower_ref, partial_ref, picker_ref, pick_ref):
    _, rows, channels, columns = frames_ref.shape
    half = columns // 2
    picker_ref[...] = column_picker(columns)
    flat = frames_ref[...].reshape(2 * rows * channels, columns)
    pick_ref[...] = product(flat, picker_ref[...]).astype(BF16).reshape(pick_ref.shape)

    def picked(frame, row):
        return pick_ref[frame, row]

    lower = product(stacked_weight(weight_ref, range(3)), gathered(picked, (1, 2, 3), half), TN)
    lower_ref[...] = jnp.maximum(lower, 0.0).astype(BF16)
    partial_ref[...] = product(stacked_weight(weight_ref, (1, 2)), gathered(picked, (0, 1), half), TN)


def step_offsets(band):
    even, odd = BAND_REACH, BAND_REACH - 1
    table = []
    for p in range(band):
        far = odd if p % 2 else even
        sign = -1 if (p % 2 + p // 2) % 2 else 1
        table.append([sign * far, sign * (far - 2), -sign * far, -sign * (far - 2)])
    return table


def held_class(band, start_ref, count_ref, offsets, slots):
    place = lax.axis_index("band")
    core = lax.rem(place, 2)
    start = start_ref[0]
    swap = lax.rem(start + 2 * BAND_REACH, 2)
    slot_of = [j * band + place - core + lax.rem(core + swap, 2) for j in range(slots)]
    steps = []
    for choices in zip(*offsets):
        step = choices[-1]
        for p in range(len(choices) - 1):
            step = jnp.where(place == p, choices[p], step)
        steps.append(step)
    return swap == 0, [start + k for k in slot_of], [k < count_ref[0] for k in slot_of], steps


def target_kernel(
    band, offsets, factor, start_ref, count_ref, rim_ref, weight_ref, lower_ref, partial_ref, picker_ref, proj_ref,
    grad_ref, other_ref, spread_ref, target_ref, scaled_ref, own_ref, *refs
):
    message_refs, tile_ref = refs[:-1], refs[-1]
    half = lower_ref.shape[1] // 2
    mid = lower_ref.shape[0]
    channels = rim_ref.shape[2]
    slots = tile_ref.shape[0]
    pick = product(rim_ref[...].reshape(2 * channels, 2 * half), picker_ref[...]).astype(BF16)

    def picked(frame, row):
        return pick[frame * channels : (frame + 1) * channels]

    upper = product(stacked_weight(weight_ref, (0,)), gathered(picked, (0,), half), TN) + partial_ref[...]
    upper = jnp.maximum(upper, 0.0).astype(BF16)
    source = jnp.concatenate([upper[:, :half], lower_ref[:, :half]], axis=1)
    target = jnp.concatenate([upper[:, half:], lower_ref[:, half:]], axis=1)
    gram = product(proj_ref[...], proj_ref[...], NT)
    both = product(jnp.concatenate(halves(gram), axis=0), source)
    high, low = halves((both[:mid] + both[mid:]) * factor)
    scaled_ref[:mid, :] = high
    scaled_ref[mid : 2 * mid, :] = low
    scaled_ref[2 * mid :, :] = high
    same, held, active, steps = held_class(band, start_ref, count_ref, offsets, slots)

    def term(slot, block_ref):
        high, low = halves(product(source, block_ref[0, slot, 0], NT))
        both = product(jnp.concatenate([high, low], axis=0), spread_ref[...])
        tile_ref[slot] = (both[:mid] + both[mid:]).astype(BF16)

    for slot in range(slots):
        pl.when(jnp.logical_and(active[slot], same))(lambda: term(slot, grad_ref))
        pl.when(jnp.logical_and(active[slot], jnp.logical_not(same)))(lambda: term(slot, other_ref))

    def chosen(offset):
        out = jnp.zeros(tile_ref.shape[1:], BF16)
        for slot in range(slots):
            out = jnp.where(jnp.logical_and(active[slot], held[slot] == offset), tile_ref[slot], out)
        return out

    target_ref[...] = target
    own_ref[...] = chosen(0)
    for step, message_ref in zip(steps, message_refs):
        message_ref[0] = target
        message_ref[1] = chosen(-step)


def gradient_kernel(
    band, offsets, factor, start_ref, count_ref, grad_ref, other_ref, spread_ref, proj_ref, target_ref, own_ref, *refs
):
    arrived, (held_ref, kept_ref, *sent_refs, sum_ref, out_ref) = refs[: len(offsets[0])], refs[len(offsets[0]) :]
    slots, mid, pixels = held_ref.shape
    same, held, active, steps = held_class(band, start_ref, count_ref, offsets, slots)
    sum_ref[...] = jnp.zeros(sum_ref.shape, F32)

    def add(slot, block_ref):
        high, low = halves(product(held_ref[slot], spread_ref[...], NT))
        both = product(jnp.concatenate([high, low], axis=0), block_ref[0, slot, 0])
        sum_ref[...] += both[:mid] + both[mid:]

    for slot in range(slots):
        block = target_ref[...]
        for step, part in zip(steps, arrived):
            block = jnp.where(held[slot] == step, part[0], block)
        held_ref[slot] = block
        pl.when(jnp.logical_and(active[slot], same))(lambda: add(slot, grad_ref))
        pl.when(jnp.logical_and(active[slot], jnp.logical_not(same)))(lambda: add(slot, other_ref))

    total = own_ref[...].astype(F32)
    for part in arrived:
        total = total + part[1].astype(F32)
    high, low = halves(jnp.concatenate([sum_ref[...], total], axis=1))
    out_ref[...] = (product(proj_ref[...], high, TN) + product(proj_ref[...], low, TN)) * factor
    parts, share, width = kept_ref.shape
    place = lax.axis_index("band")
    for k in range(band):
        first = pl.multiple_of(jnp.bitwise_xor(place, k) * share, share)
        for part in range(parts):
            out = out_ref[pl.ds(first, share), part * width : (part + 1) * width]
            if k == 0:
                kept_ref[part] = out
            else:
                sent_refs[k - 1][part] = out.astype(BF16)


def pyramid_kernel(band, start_ref, count_ref, held_ref, other_ref, scaled_ref, spread_ref, pyramid_ref):
    slot = pl.program_id(0)
    active = slot * band + lax.axis_index("band") < count_ref[0]
    same = lax.rem(start_ref[0] + 2 * BAND_REACH, 2) == 0

    @pl.when(active)
    def _():
        target = jnp.where(same, held_ref[0], other_ref[0])
        high, low = halves(product(spread_ref[...], target, NT))
        corr = product(jnp.concatenate([high, high, low], axis=1), scaled_ref[...])
        pyramid_ref[0, 0, 0] = corr.astype(BF16)

    @pl.when(jnp.logical_not(active))
    def _():
        pyramid_ref[0, 0, 0] = jnp.zeros(pyramid_ref.shape[3:], BF16)


def shards(frames, conv_weight, proj_weight, band_start, band_count, pyramid_grad):
    band = lax.axis_size("band")
    row_blocks = lax.axis_size("rows")
    mid, channels = proj_weight.shape
    share = channels // band
    factor = 1.0 / math.sqrt(channels)
    frames = jnp.swapaxes(frames, 2, 3)
    grad = jnp.swapaxes(pyramid_grad, 3, 4)
    slots = grad.shape[1]
    entries, pixels = grad.shape[3:]
    columns = frames.shape[3]
    half = columns // 2
    params = pltpu.CompilerParams(vmem_limit_bytes=VMEM_LIMIT)
    smem = pl.BlockSpec(memory_space=pltpu.SMEM)
    vmem = pl.BlockSpec(memory_space=pltpu.VMEM)
    spread = jnp.asarray(spread_matrix(pixels))

    offsets = step_offsets(band)
    steps = len(offsets[0])

    def along_rows(x, step):
        pairs = []
        for row in range(row_blocks):
            for p in range(band):
                to = row - offsets[p][step]
                if 0 <= to < row_blocks:
                    pairs.append((row * band + p, to * band + p))
        return lax.ppermute(x, ("rows", "band"), pairs)

    def across(x, k):
        return lax.ppermute(x, "band", [(p, p ^ k) for p in range(band)])

    rim = lax.ppermute(frames[:, -1:], "rows", [(i, i + 1) for i in range(row_blocks - 1)])
    other_grad = across(grad, 1)
    lower, partial, picker = pl.pallas_call(
        local_rows_kernel,
        out_shape=(
            jax.ShapeDtypeStruct((mid, columns), BF16),
            jax.ShapeDtypeStruct((mid, columns), F32),
            jax.ShapeDtypeStruct((columns, 3 * half), BF16),
        ),
        scratch_shapes=[pltpu.VMEM(frames.shape[:3] + (3 * half,), BF16)],
        compiler_params=params,
        cost_estimate=pl.CostEstimate(flops=2**31, bytes_accessed=2**21, transcendentals=0),
    )(frames, conv_weight)

    block = jax.ShapeDtypeStruct((mid, pixels), BF16)
    message = jax.ShapeDtypeStruct((2, mid, pixels), BF16)
    target, scaled, own_term, *messages = pl.pallas_call(
        lambda *refs: target_kernel(band, offsets, factor, *refs),
        in_specs=[smem] * 2 + [vmem] * 9,
        out_shape=(block, jax.ShapeDtypeStruct((3 * mid, pixels), BF16), block) + (message,) * steps,
        scratch_shapes=[pltpu.VMEM((slots, mid, pixels), BF16)],
        compiler_params=params,
        cost_estimate=pl.CostEstimate(flops=2**31, bytes_accessed=2**22, transcendentals=0),
    )(band_start, band_count, rim, conv_weight, lower, partial, picker, proj_weight, grad, other_grad, spread)

    arrived = [along_rows(messages[i], i) for i in range(steps)]

    out_parts = 2 * pixels // half
    part = (out_parts, share, half)
    held, kept, *sent = pl.pallas_call(
        lambda *refs: gradient_kernel(band, offsets, factor, *refs),
        in_specs=[smem] * 2 + [vmem] * (6 + steps),
        out_shape=(jax.ShapeDtypeStruct((slots, mid, pixels), BF16), jax.ShapeDtypeStruct(part, F32))
        + (jax.ShapeDtypeStruct(part, BF16),) * (band - 1),
        scratch_shapes=[pltpu.VMEM((mid, pixels), F32), pltpu.VMEM((channels, 2 * pixels), F32)],
        compiler_params=params,
        cost_estimate=pl.CostEstimate(flops=2**31, bytes_accessed=2**22, transcendentals=0),
    )(band_start, band_count, grad, other_grad, spread, proj_weight, target, own_term, *arrived)

    received = [across(sent[k - 1], k) for k in reversed(range(1, band))]
    other = across(held, 1)

    def whole(shape):
        return pl.BlockSpec(shape, lambda j: (0,) * len(shape))

    target_spec = pl.BlockSpec((1, mid, pixels), lambda j: (j, 0, 0))
    grad_spec = pl.BlockSpec((1, 1, 1, entries, pixels), lambda j: (0, j, 0, 0, 0))
    pyramid = pl.pallas_call(
        lambda *refs: pyramid_kernel(band, *refs),
        grid=(slots,),
        in_specs=[smem, smem, target_spec, target_spec, whole((3 * mid, pixels)), whole((entries, pixels))],
        out_specs=grad_spec,
        out_shape=jax.ShapeDtypeStruct(grad.shape, BF16),
        compiler_params=params,
        cost_estimate=pl.CostEstimate(flops=2**31, bytes_accessed=2**22, transcendentals=0),
    )(band_start, band_count, held, other, scaled, spread)

    total, pyramid = lax.optimization_barrier((kept, pyramid))
    for x in received:
        total = total + x.astype(F32)
    total = jnp.swapaxes(total, 1, 2)
    return (jnp.swapaxes(pyramid, 3, 4), total[: out_parts // 2], total[out_parts // 2 :])


def solution(mesh):
    in_specs = (
        P(None, "rows", None, None),
        P(),
        P(),
        P("rows"),
        P("rows"),
        P("rows", None, "band", None, None),
    )
    out_specs = (
        P("rows", None, "band", None, None),
        P("rows", None, "band"),
        P("rows", None, "band"),
    )
    return jax.shard_map(shards, mesh=mesh, in_specs=in_specs, out_specs=out_specs, check_vma=False)
```

```python
import math

import jax
import jax.numpy as jnp
import numpy as np
from jax import lax
from jax.experimental import pallas as pl
from jax.experimental.pallas import tpu as pltpu
from jax.sharding import PartitionSpec as P

LEVELS = 4
BAND_REACH = 4
F32 = jnp.float32
BF16 = jnp.bfloat16
VMEM_LIMIT = 28 * 1024 * 1024
NN = (((1,), (0,)), ((), ()))
NT = (((1,), (1,)), ((), ()))
TN = (((0,), (0,)), ((), ()))


def product(a, b, dims=NN):
    return lax.dot_general(a, b, dims, preferred_element_type=F32)


def halves(x):
    high = x.astype(BF16)
    return high, (x - high.astype(F32)).astype(BF16)


def spread_matrix(pixels):
    parts = []
    for level in range(LEVELS):
        group = 2**level
        parts.append(np.repeat(np.eye(pixels // group, dtype=np.float32), group, axis=1) / group)
    return np.concatenate(parts, axis=0).astype(jnp.bfloat16)


def column_picker(columns):
    half = columns // 2
    taps = [
        (
            lax.broadcasted_iota(jnp.int32, (columns, half), 0)
            == 2 * lax.broadcasted_iota(jnp.int32, (columns, half), 1) + (dx - 1)
        )
        for dx in range(3)
    ]
    return jnp.concatenate([jnp.where(tap, 1.0, 0.0).astype(BF16) for tap in taps], axis=1)


def gathered(picked, rows, half):
    return jnp.concatenate(
        [
            jnp.concatenate([picked(frame, row)[:, dx * half : (dx + 1) * half] for frame in range(2)], axis=1)
            for row in rows
            for dx in range(3)
        ],
        axis=0,
    )


def stacked_weight(weight_ref, taps):
    return jnp.concatenate([weight_ref[dy, dx] for dy in taps for dx in range(3)], axis=0)


def picker_kernel(picker_ref):
    picker_ref[...] = column_picker(picker_ref.shape[0])


def local_rows_kernel(picker_ref, frames_ref, weight_ref, lower_ref, partial_ref, pick_ref):
    _, rows, channels, columns = frames_ref.shape
    half = columns // 2
    flat = frames_ref[...].reshape(2 * rows * channels, columns)
    pick_ref[...] = product(flat, picker_ref[...]).astype(BF16).reshape(pick_ref.shape)

    def picked(frame, row):
        return pick_ref[frame, row]

    lower = product(stacked_weight(weight_ref, range(3)), gathered(picked, (1, 2, 3), half), TN)
    lower_ref[...] = jnp.maximum(lower, 0.0).astype(BF16)
    partial_ref[...] = product(stacked_weight(weight_ref, (1, 2)), gathered(picked, (0, 1), half), TN)


def step_table(band):
    even = [(4, 0), (2, 0), (2, 1), (4, 1)]
    odd = [(3, 0), (1, 0), (3, 1), (1, 1)]
    table = [even, odd]
    return [table[p % len(table)] for p in range(band)]


SPLIT_BLOCKS = (0,)
SPLIT_TERMS = (2, 3)


def pixel_halves(block):
    width = block.shape[1] // 2
    return block[:, :width], block[:, width:]


def own_half(block, swapped=False):
    first, second = pixel_halves(block)
    return jnp.where((lax.div(lax.axis_index("band"), 2) == 0) != swapped, first, second)


def joined(mine, others):
    is_first = lax.div(lax.axis_index("band"), 2) == 0
    return jnp.concatenate([jnp.where(is_first, mine, others), jnp.where(is_first, others, mine)], axis=1)


def held_class(band, start_ref, count_ref, table, slots):
    place = lax.axis_index("band")
    core = lax.rem(place, 2)
    start = start_ref[0]
    swap = lax.rem(start + 2 * BAND_REACH, 2)
    slot_of = [j * band + place - core + lax.rem(core + swap, 2) for j in range(slots)]
    row = lax.axis_index("rows")
    steps = []
    for choices in zip(*table):
        step = 0
        for p, (distance, turn) in enumerate(choices):
            lower = lax.rem(lax.div(row, distance), 2) == turn
            step = jnp.where(place == p, jnp.where(lower, distance, -distance), step)
        steps.append(step)
    return swap == 0, [start + k for k in slot_of], [k < count_ref[0] for k in slot_of], steps


def target_kernel(
    band, table, factor, start_ref, count_ref, rim_ref, weight_ref, lower_ref, partial_ref, picker_ref, proj_ref,
    grad_ref, other_ref, spread_ref, target_ref, scaled_ref, own_ref, kept_ref, crossing_ref, *refs
):
    message_refs, tile_ref = refs[:-1], refs[-1]
    half = lower_ref.shape[1] // 2
    mid = lower_ref.shape[0]
    channels = rim_ref.shape[2]
    slots = tile_ref.shape[0]
    pick = product(rim_ref[...].reshape(2 * channels, 2 * half), picker_ref[...]).astype(BF16)

    def picked(frame, row):
        return pick[frame * channels : (frame + 1) * channels]

    upper = product(stacked_weight(weight_ref, (0,)), gathered(picked, (0,), half), TN) + partial_ref[...]
    upper = jnp.maximum(upper, 0.0).astype(BF16)
    source = jnp.concatenate([upper[:, :half], lower_ref[:, :half]], axis=1)
    target = jnp.concatenate([upper[:, half:], lower_ref[:, half:]], axis=1)
    gram = product(proj_ref[...], proj_ref[...], NT)
    both = product(jnp.concatenate(halves(gram), axis=0), source)
    high, low = halves((both[:mid] + both[mid:]) * factor)
    scaled_ref[:mid, :] = high
    scaled_ref[mid : 2 * mid, :] = low
    scaled_ref[2 * mid :, :] = high
    same, held, active, steps = held_class(band, start_ref, count_ref, table, slots)

    def term(slot, block_ref):
        high, low = halves(product(source, block_ref[0, slot, 0], NT))
        both = product(jnp.concatenate([high, low], axis=0), spread_ref[...])
        tile_ref[slot] = (both[:mid] + both[mid:]).astype(BF16)

    for slot in range(slots):
        pl.when(jnp.logical_and(active[slot], same))(lambda: term(slot, grad_ref))
        pl.when(jnp.logical_and(active[slot], jnp.logical_not(same)))(lambda: term(slot, other_ref))

    def chosen(offset):
        out = jnp.zeros(tile_ref.shape[1:], BF16)
        for slot in range(slots):
            out = jnp.where(jnp.logical_and(active[slot], held[slot] == offset), tile_ref[slot], out)
        return out

    target_ref[...] = target
    own_ref[...] = chosen(0)
    for i, (step, message_ref) in enumerate(zip(steps, message_refs)):
        blocks = [own_half(target)] if i in SPLIT_BLOCKS else pixel_halves(target)
        tile = chosen(step)
        if i in SPLIT_TERMS:
            kept_ref[SPLIT_TERMS.index(i)] = own_half(tile)
            crossing_ref[SPLIT_TERMS.index(i)] = own_half(tile, True)
        else:
            blocks = [*blocks, *pixel_halves(tile)]
        for j, part in enumerate(blocks):
            message_ref[j] = part


def gradient_kernel(
    band, table, factor, start_ref, count_ref, grad_ref, other_ref, spread_ref, proj_ref, target_ref, own_ref, *refs
):
    arrived, others, (held_ref, kept_ref, *sent_refs, sum_ref, out_ref) = (
        refs[: len(table[0])],
        refs[len(table[0]) : len(table[0]) + len(SPLIT_BLOCKS)],
        refs[len(table[0]) + len(SPLIT_BLOCKS) :],
    )
    slots, mid, pixels = held_ref.shape
    same, held, active, steps = held_class(band, start_ref, count_ref, table, slots)
    sum_ref[...] = jnp.zeros(sum_ref.shape, F32)

    def add(slot, block_ref):
        high, low = halves(product(held_ref[slot], spread_ref[...], NT))
        both = product(jnp.concatenate([high, low], axis=0), block_ref[0, slot, 0])
        sum_ref[...] += both[:mid] + both[mid:]

    for slot in range(slots):
        block = target_ref[...]
        for i, (step, part) in enumerate(zip(steps, arrived)):
            if i in SPLIT_BLOCKS:
                came = joined(part[0], others[SPLIT_BLOCKS.index(i)][...])
            else:
                came = jnp.concatenate([part[0], part[1]], axis=1)
            block = jnp.where(held[slot] == step, came, block)
        held_ref[slot] = block
        pl.when(jnp.logical_and(active[slot], same))(lambda: add(slot, grad_ref))
        pl.when(jnp.logical_and(active[slot], jnp.logical_not(same)))(lambda: add(slot, other_ref))

    total = own_ref[...].astype(F32)
    nothing = jnp.zeros((mid, pixels // 2), BF16)
    for i, part in enumerate(arrived):
        last = part.shape[0] - 1
        if i in SPLIT_TERMS:
            came = joined(part[last], nothing)
        else:
            came = jnp.concatenate([part[last - 1], part[last]], axis=1)
        total = total + came.astype(F32)
    high, low = halves(jnp.concatenate([sum_ref[...], total], axis=1))
    out_ref[...] = (product(proj_ref[...], high, TN) + product(proj_ref[...], low, TN)) * factor
    parts, share, width = kept_ref.shape
    place = lax.axis_index("band")
    for k in range(band):
        first = pl.multiple_of(jnp.bitwise_xor(place, k) * share, share)
        for part in range(parts):
            out = out_ref[pl.ds(first, share), part * width : (part + 1) * width]
            if k == 0:
                kept_ref[part] = out
            else:
                sent_refs[k - 1][part] = out.astype(BF16)


def pyramid_kernel(band, start_ref, count_ref, held_ref, other_ref, scaled_ref, spread_ref, pyramid_ref):
    slot = pl.program_id(0)
    active = slot * band + lax.axis_index("band") < count_ref[0]
    same = lax.rem(start_ref[0] + 2 * BAND_REACH, 2) == 0

    @pl.when(active)
    def _():
        target = jnp.where(same, held_ref[0], other_ref[0])
        high, low = halves(product(spread_ref[...], target, NT))
        corr = product(jnp.concatenate([high, high, low], axis=1), scaled_ref[...])
        pyramid_ref[0, 0, 0] = corr.astype(BF16)

    @pl.when(jnp.logical_not(active))
    def _():
        pyramid_ref[0, 0, 0] = jnp.zeros(pyramid_ref.shape[3:], BF16)


def shards(frames, conv_weight, proj_weight, band_start, band_count, pyramid_grad):
    band = lax.axis_size("band")
    row_blocks = lax.axis_size("rows")
    mid, channels = proj_weight.shape
    share = channels // band
    factor = 1.0 / math.sqrt(channels)
    frames = jnp.swapaxes(frames, 2, 3)
    grad = jnp.swapaxes(pyramid_grad, 3, 4)
    slots = grad.shape[1]
    entries, pixels = grad.shape[3:]
    columns = frames.shape[3]
    half = columns // 2
    params = pltpu.CompilerParams(vmem_limit_bytes=VMEM_LIMIT)
    smem = pl.BlockSpec(memory_space=pltpu.SMEM)
    vmem = pl.BlockSpec(memory_space=pltpu.VMEM)
    spread = jnp.asarray(spread_matrix(pixels))

    table = step_table(band)
    steps = len(table[0])

    def along_rows(x, step):
        pairs = []
        for p in range(band):
            distance, turn = table[p][step]
            for row in range(row_blocks - distance):
                if row // distance % 2 == turn:
                    pairs.append((row * band + p, (row + distance) * band + p))
                    pairs.append(((row + distance) * band + p, row * band + p))
        return lax.ppermute(x, ("rows", "band"), pairs)

    def across(x, k):
        return lax.ppermute(x, "band", [(p, p ^ k) for p in range(band)])

    rim = lax.ppermute(frames[:, -1:], "rows", [(i, i + 1) for i in range(row_blocks - 1)])
    other_grad = across(grad, 1)
    picker = pl.pallas_call(
        picker_kernel,
        out_shape=jax.ShapeDtypeStruct((columns, 3 * half), BF16),
        compiler_params=params,
        cost_estimate=pl.CostEstimate(flops=2**33, bytes_accessed=2**21, transcendentals=0),
    )()
    lower, partial = pl.pallas_call(
        local_rows_kernel,
        out_shape=(
            jax.ShapeDtypeStruct((mid, columns), BF16),
            jax.ShapeDtypeStruct((mid, columns), F32),
        ),
        scratch_shapes=[pltpu.VMEM(frames.shape[:3] + (3 * half,), BF16)],
        compiler_params=params,
        cost_estimate=pl.CostEstimate(flops=2**31, bytes_accessed=2**21, transcendentals=0),
    )(picker, frames, conv_weight)

    block = jax.ShapeDtypeStruct((mid, pixels), BF16)
    piece = (mid, pixels // 2)
    crossing = jax.ShapeDtypeStruct((len(SPLIT_TERMS),) + piece, BF16)
    messages = [
        jax.ShapeDtypeStruct(((1 if i in SPLIT_BLOCKS else 2) + (0 if i in SPLIT_TERMS else 2),) + piece, BF16)
        for i in range(steps)
    ]
    target, scaled, own_term, terms, crossing, *messages = pl.pallas_call(
        lambda *refs: target_kernel(band, table, factor, *refs),
        in_specs=[smem] * 2 + [vmem] * 9,
        out_shape=(block, jax.ShapeDtypeStruct((3 * mid, pixels), BF16), block, crossing, crossing, *messages),
        scratch_shapes=[pltpu.VMEM((slots, mid, pixels), BF16)],
        compiler_params=params,
        cost_estimate=pl.CostEstimate(flops=2**31, bytes_accessed=2**22, transcendentals=0),
    )(band_start, band_count, rim, conv_weight, lower, partial, picker, proj_weight, grad, other_grad, spread)

    others = across(crossing, 2)
    for j, i in enumerate(SPLIT_TERMS):
        messages[i] = jnp.concatenate([messages[i], terms[j : j + 1] + others[j : j + 1]])
    arrived = [along_rows(messages[i], i) for i in range(steps)]
    other_blocks = [across(arrived[i][0], 2) for i in SPLIT_BLOCKS]

    out_parts = 2 * pixels // half
    part = (out_parts, share, half)
    held, kept, *sent = pl.pallas_call(
        lambda *refs: gradient_kernel(band, table, factor, *refs),
        in_specs=[smem] * 2 + [vmem] * (6 + steps + len(SPLIT_BLOCKS)),
        out_shape=(jax.ShapeDtypeStruct((slots, mid, pixels), BF16), jax.ShapeDtypeStruct(part, F32))
        + (jax.ShapeDtypeStruct(part, BF16),) * (band - 1),
        scratch_shapes=[pltpu.VMEM((mid, pixels), F32), pltpu.VMEM((channels, 2 * pixels), F32)],
        compiler_params=params,
        cost_estimate=pl.CostEstimate(flops=2**31, bytes_accessed=2**22, transcendentals=0),
    )(band_start, band_count, grad, other_grad, spread, proj_weight, target, own_term, *arrived, *other_blocks)

    received = [across(sent[k - 1], k) for k in reversed(range(1, band))]
    other = across(held, 1)

    def whole(shape):
        return pl.BlockSpec(shape, lambda j: (0,) * len(shape))

    target_spec = pl.BlockSpec((1, mid, pixels), lambda j: (j, 0, 0))
    grad_spec = pl.BlockSpec((1, 1, 1, entries, pixels), lambda j: (0, j, 0, 0, 0))
    pyramid = pl.pallas_call(
        lambda *refs: pyramid_kernel(band, *refs),
        grid=(slots,),
        in_specs=[smem, smem, target_spec, target_spec, whole((3 * mid, pixels)), whole((entries, pixels))],
        out_specs=grad_spec,
        out_shape=jax.ShapeDtypeStruct(grad.shape, BF16),
        compiler_params=params,
        cost_estimate=pl.CostEstimate(flops=2**31, bytes_accessed=2**22, transcendentals=0),
    )(band_start, band_count, held, other, scaled, spread)

    total, pyramid = lax.optimization_barrier((kept, pyramid))
    for x in received:
        total = total + x.astype(F32)
    total = jnp.swapaxes(total, 1, 2)
    return (jnp.swapaxes(pyramid, 3, 4), total[: out_parts // 2], total[out_parts // 2 :])


def solution(mesh):
    in_specs = (
        P(None, "rows", None, None),
        P(),
        P(),
        P("rows"),
        P("rows"),
        P("rows", None, "band", None, None),
    )
    out_specs = (
        P("rows", None, "band", None, None),
        P("rows", None, "band"),
        P("rows", None, "band"),
    )
    return jax.shard_map(shards, mesh=mesh, in_specs=in_specs, out_specs=out_specs, check_vma=False)
```

```python
import math

import jax
import jax.numpy as jnp
import numpy as np
from jax import lax
from jax.experimental import pallas as pl
from jax.experimental.pallas import tpu as pltpu
from jax.sharding import PartitionSpec as P

LEVELS = 4
BAND_REACH = 4
F32 = jnp.float32
BF16 = jnp.bfloat16
VMEM_LIMIT = 28 * 1024 * 1024
NN = (((1,), (0,)), ((), ()))
NT = (((1,), (1,)), ((), ()))
TN = (((0,), (0,)), ((), ()))


def product(a, b, dims=NN):
    return lax.dot_general(a, b, dims, preferred_element_type=F32)


def halves(x):
    high = x.astype(BF16)
    return high, (x - high.astype(F32)).astype(BF16)


def spread_matrix(pixels):
    parts = []
    for level in range(LEVELS):
        group = 2**level
        parts.append(np.repeat(np.eye(pixels // group, dtype=np.float32), group, axis=1) / group)
    return np.concatenate(parts, axis=0).astype(jnp.bfloat16)


def column_picker(columns):
    half = columns // 2
    taps = [
        (
            lax.broadcasted_iota(jnp.int32, (columns, half), 0)
            == 2 * lax.broadcasted_iota(jnp.int32, (columns, half), 1) + (dx - 1)
        )
        for dx in range(3)
    ]
    return jnp.concatenate([jnp.where(tap, 1.0, 0.0).astype(BF16) for tap in taps], axis=1)


def gathered(picked, rows, half):
    return jnp.concatenate(
        [
            jnp.concatenate([picked(frame, row)[:, dx * half : (dx + 1) * half] for frame in range(2)], axis=1)
            for row in rows
            for dx in range(3)
        ],
        axis=0,
    )


def stacked_weight(weight_ref, taps):
    return jnp.concatenate([weight_ref[dy, dx] for dy in taps for dx in range(3)], axis=0)


def picker_kernel(picker_ref):
    picker_ref[...] = column_picker(picker_ref.shape[0])


def local_rows_kernel(picker_ref, frames_ref, weight_ref, lower_ref, partial_ref, pick_ref):
    _, rows, channels, columns = frames_ref.shape
    half = columns // 2
    flat = frames_ref[...].reshape(2 * rows * channels, columns)
    pick_ref[...] = product(flat, picker_ref[...]).astype(BF16).reshape(pick_ref.shape)

    def picked(frame, row):
        return pick_ref[frame, row]

    lower = product(stacked_weight(weight_ref, range(3)), gathered(picked, (1, 2, 3), half), TN)
    lower_ref[...] = jnp.maximum(lower, 0.0).astype(BF16)
    partial_ref[...] = product(stacked_weight(weight_ref, (1, 2)), gathered(picked, (0, 1), half), TN)


def step_table(band):
    even = [(4, 0), (2, 0), (2, 1), (4, 1)]
    odd = [(1, 1), (1, 0), (3, 0), (3, 1)]
    table = [even, odd]
    return [table[p % len(table)] for p in range(band)]


SPLIT_BLOCKS = (0,)
SPLIT_TERMS = (2, 3)


def pixel_halves(block):
    width = block.shape[1] // 2
    return block[:, :width], block[:, width:]


def own_half(block, swapped=False):
    first, second = pixel_halves(block)
    return jnp.where((lax.div(lax.axis_index("band"), 2) == 0) != swapped, first, second)


def joined(mine, others):
    is_first = lax.div(lax.axis_index("band"), 2) == 0
    return jnp.concatenate([jnp.where(is_first, mine, others), jnp.where(is_first, others, mine)], axis=1)


def held_class(band, start_ref, count_ref, table, slots):
    place = lax.axis_index("band")
    core = lax.rem(place, 2)
    start = start_ref[0]
    swap = lax.rem(start + 2 * BAND_REACH, 2)
    slot_of = [j * band + place - core + lax.rem(core + swap, 2) for j in range(slots)]
    row = lax.axis_index("rows")
    steps = []
    for choices in zip(*table):
        step = 0
        for p, (distance, turn) in enumerate(choices):
            lower = lax.rem(lax.div(row, distance), 2) == turn
            step = jnp.where(place == p, jnp.where(lower, distance, -distance), step)
        steps.append(step)
    return swap == 0, [start + k for k in slot_of], [k < count_ref[0] for k in slot_of], steps


def target_kernel(
    band, table, factor, start_ref, count_ref, rim_ref, weight_ref, lower_ref, partial_ref, picker_ref, proj_ref,
    grad_ref, other_ref, spread_ref, target_ref, scaled_ref, own_ref, terms_ref, *refs
):
    message_refs, tile_ref = refs[:-1], refs[-1]
    half = lower_ref.shape[1] // 2
    mid = lower_ref.shape[0]
    channels = rim_ref.shape[2]
    slots = tile_ref.shape[0]
    pick = product(rim_ref[...].reshape(2 * channels, 2 * half), picker_ref[...]).astype(BF16)

    def picked(frame, row):
        return pick[frame * channels : (frame + 1) * channels]

    upper = product(stacked_weight(weight_ref, (0,)), gathered(picked, (0,), half), TN) + partial_ref[...]
    upper = jnp.maximum(upper, 0.0).astype(BF16)
    source = jnp.concatenate([upper[:, :half], lower_ref[:, :half]], axis=1)
    target = jnp.concatenate([upper[:, half:], lower_ref[:, half:]], axis=1)
    gram = product(proj_ref[...], proj_ref[...], NT)
    both = product(jnp.concatenate(halves(gram), axis=0), source)
    high, low = halves((both[:mid] + both[mid:]) * factor)
    scaled_ref[:mid, :] = high
    scaled_ref[mid : 2 * mid, :] = low
    scaled_ref[2 * mid :, :] = high
    same, held, active, steps = held_class(band, start_ref, count_ref, table, slots)

    def term(slot, block_ref):
        high, low = halves(product(source, block_ref[0, slot, 0], NT))
        both = product(jnp.concatenate([high, low], axis=0), spread_ref[...])
        tile_ref[slot] = (both[:mid] + both[mid:]).astype(BF16)

    for slot in range(slots):
        pl.when(jnp.logical_and(active[slot], same))(lambda: term(slot, grad_ref))
        pl.when(jnp.logical_and(active[slot], jnp.logical_not(same)))(lambda: term(slot, other_ref))

    def chosen(offset):
        out = jnp.zeros(tile_ref.shape[1:], BF16)
        for slot in range(slots):
            out = jnp.where(jnp.logical_and(active[slot], held[slot] == offset), tile_ref[slot], out)
        return out

    target_ref[...] = target
    own_ref[...] = chosen(0)
    for i, (step, message_ref) in enumerate(zip(steps, message_refs)):
        blocks = [own_half(target)] if i in SPLIT_BLOCKS else pixel_halves(target)
        tile = chosen(step)
        if i in SPLIT_TERMS:
            for j, part in enumerate(pixel_halves(tile)):
                terms_ref[SPLIT_TERMS.index(i), j] = part
        else:
            blocks = [*blocks, *pixel_halves(tile)]
        for j, part in enumerate(blocks):
            message_ref[j] = part


def gradient_kernel(
    band, table, factor, start_ref, count_ref, grad_ref, other_ref, spread_ref, proj_ref, target_ref, own_ref, *refs
):
    arrived, others, (held_ref, kept_ref, *sent_refs, sum_ref, out_ref) = (
        refs[: len(table[0])],
        refs[len(table[0]) : len(table[0]) + len(SPLIT_BLOCKS)],
        refs[len(table[0]) + len(SPLIT_BLOCKS) :],
    )
    slots, mid, pixels = held_ref.shape
    same, held, active, steps = held_class(band, start_ref, count_ref, table, slots)
    sum_ref[...] = jnp.zeros(sum_ref.shape, F32)

    def add(slot, block_ref):
        high, low = halves(product(held_ref[slot], spread_ref[...], NT))
        both = product(jnp.concatenate([high, low], axis=0), block_ref[0, slot, 0])
        sum_ref[...] += both[:mid] + both[mid:]

    for slot in range(slots):
        block = target_ref[...]
        for i, (step, part) in enumerate(zip(steps, arrived)):
            if i in SPLIT_BLOCKS:
                came = joined(part[0], others[SPLIT_BLOCKS.index(i)][...])
            else:
                came = jnp.concatenate([part[0], part[1]], axis=1)
            block = jnp.where(held[slot] == step, came, block)
        held_ref[slot] = block
        pl.when(jnp.logical_and(active[slot], same))(lambda: add(slot, grad_ref))
        pl.when(jnp.logical_and(active[slot], jnp.logical_not(same)))(lambda: add(slot, other_ref))

    total = own_ref[...].astype(F32)
    nothing = jnp.zeros((mid, pixels // 2), BF16)
    for i, part in enumerate(arrived):
        last = part.shape[0] - 1
        if i in SPLIT_TERMS:
            came = joined(part[last], nothing)
        else:
            came = jnp.concatenate([part[last - 1], part[last]], axis=1)
        total = total + came.astype(F32)
    high, low = halves(jnp.concatenate([sum_ref[...], total], axis=1))
    out_ref[...] = (product(proj_ref[...], high, TN) + product(proj_ref[...], low, TN)) * factor
    parts, share, width = kept_ref.shape
    place = lax.axis_index("band")
    for k in range(band):
        first = pl.multiple_of(jnp.bitwise_xor(place, k) * share, share)
        for part in range(parts):
            out = out_ref[pl.ds(first, share), part * width : (part + 1) * width]
            if k == 0:
                kept_ref[part] = out
            else:
                sent_refs[k - 1][part] = out.astype(BF16)


def pyramid_kernel(band, start_ref, count_ref, held_ref, other_ref, scaled_ref, spread_ref, pyramid_ref):
    slot = pl.program_id(0)
    active = slot * band + lax.axis_index("band") < count_ref[0]
    same = lax.rem(start_ref[0] + 2 * BAND_REACH, 2) == 0

    @pl.when(active)
    def _():
        target = jnp.where(same, held_ref[0], other_ref[0])
        high, low = halves(product(spread_ref[...], target, NT))
        corr = product(jnp.concatenate([high, high, low], axis=1), scaled_ref[...])
        pyramid_ref[0, 0, 0] = corr.astype(BF16)

    @pl.when(jnp.logical_not(active))
    def _():
        pyramid_ref[0, 0, 0] = jnp.zeros(pyramid_ref.shape[3:], BF16)


def shards(frames, conv_weight, proj_weight, band_start, band_count, pyramid_grad):
    band = lax.axis_size("band")
    row_blocks = lax.axis_size("rows")
    mid, channels = proj_weight.shape
    share = channels // band
    factor = 1.0 / math.sqrt(channels)
    frames = jnp.swapaxes(frames, 2, 3)
    grad = jnp.swapaxes(pyramid_grad, 3, 4)
    slots = grad.shape[1]
    entries, pixels = grad.shape[3:]
    columns = frames.shape[3]
    half = columns // 2
    params = pltpu.CompilerParams(vmem_limit_bytes=VMEM_LIMIT)
    smem = pl.BlockSpec(memory_space=pltpu.SMEM)
    vmem = pl.BlockSpec(memory_space=pltpu.VMEM)
    spread = jnp.asarray(spread_matrix(pixels))

    table = step_table(band)
    steps = len(table[0])

    def along_rows(x, step):
        pairs = []
        for p in range(band):
            distance, turn = table[p][step]
            for row in range(row_blocks - distance):
                if row // distance % 2 == turn:
                    pairs.append((row * band + p, (row + distance) * band + p))
                    pairs.append(((row + distance) * band + p, row * band + p))
        return lax.ppermute(x, ("rows", "band"), pairs)

    def across(x, k):
        return lax.ppermute(x, "band", [(p, p ^ k) for p in range(band)])

    rim = lax.ppermute(frames[:, -1:], "rows", [(i, i + 1) for i in range(row_blocks - 1)])
    other_grad = across(grad, 1)
    picker = pl.pallas_call(
        picker_kernel,
        out_shape=jax.ShapeDtypeStruct((columns, 3 * half), BF16),
        compiler_params=params,
        cost_estimate=pl.CostEstimate(flops=2**33, bytes_accessed=2**21, transcendentals=0),
    )()
    lower, partial = pl.pallas_call(
        local_rows_kernel,
        out_shape=(
            jax.ShapeDtypeStruct((mid, columns), BF16),
            jax.ShapeDtypeStruct((mid, columns), F32),
        ),
        scratch_shapes=[pltpu.VMEM(frames.shape[:3] + (3 * half,), BF16)],
        compiler_params=params,
        cost_estimate=pl.CostEstimate(flops=2**31, bytes_accessed=2**21, transcendentals=0),
    )(picker, frames, conv_weight)

    block = jax.ShapeDtypeStruct((mid, pixels), BF16)
    piece = (mid, pixels // 2)
    split_terms = jax.ShapeDtypeStruct((len(SPLIT_TERMS), 2) + piece, BF16)
    messages = [
        jax.ShapeDtypeStruct(((1 if i in SPLIT_BLOCKS else 2) + (0 if i in SPLIT_TERMS else 2),) + piece, BF16)
        for i in range(steps)
    ]
    target, scaled, own_term, terms, *messages = pl.pallas_call(
        lambda *refs: target_kernel(band, table, factor, *refs),
        in_specs=[smem] * 2 + [vmem] * 9,
        out_shape=(block, jax.ShapeDtypeStruct((3 * mid, pixels), BF16), block, split_terms, *messages),
        scratch_shapes=[pltpu.VMEM((slots, mid, pixels), BF16)],
        compiler_params=params,
        cost_estimate=pl.CostEstimate(flops=2**31, bytes_accessed=2**22, transcendentals=0),
    )(band_start, band_count, rim, conv_weight, lower, partial, picker, proj_weight, grad, other_grad, spread)

    first = lax.axis_index("band") // 2 == 0
    others = across(jnp.where(first, terms[:, 1], terms[:, 0]), 2)
    terms = jnp.where(first, terms[:, 0], terms[:, 1])
    for j, i in enumerate(SPLIT_TERMS):
        messages[i] = jnp.concatenate([messages[i], terms[j : j + 1] + others[j : j + 1]])
    arrived = [along_rows(messages[i], i) for i in range(steps)]
    other_blocks = [across(arrived[i][0], 2) for i in SPLIT_BLOCKS]

    out_parts = 2 * pixels // half
    part = (out_parts, share, half)
    held, kept, *sent = pl.pallas_call(
        lambda *refs: gradient_kernel(band, table, factor, *refs),
        in_specs=[smem] * 2 + [vmem] * (6 + steps + len(SPLIT_BLOCKS)),
        out_shape=(jax.ShapeDtypeStruct((slots, mid, pixels), BF16), jax.ShapeDtypeStruct(part, F32))
        + (jax.ShapeDtypeStruct(part, BF16),) * (band - 1),
        scratch_shapes=[pltpu.VMEM((mid, pixels), F32), pltpu.VMEM((channels, 2 * pixels), F32)],
        compiler_params=params,
        cost_estimate=pl.CostEstimate(flops=2**31, bytes_accessed=2**22, transcendentals=0),
    )(band_start, band_count, grad, other_grad, spread, proj_weight, target, own_term, *arrived, *other_blocks)

    received = [across(sent[k - 1], k) for k in reversed(range(1, band))]
    other = across(held, 1)

    def whole(shape):
        return pl.BlockSpec(shape, lambda j: (0,) * len(shape))

    target_spec = pl.BlockSpec((1, mid, pixels), lambda j: (j, 0, 0))
    grad_spec = pl.BlockSpec((1, 1, 1, entries, pixels), lambda j: (0, j, 0, 0, 0))
    pyramid = pl.pallas_call(
        lambda *refs: pyramid_kernel(band, *refs),
        grid=(slots,),
        in_specs=[smem, smem, target_spec, target_spec, whole((3 * mid, pixels)), whole((entries, pixels))],
        out_specs=grad_spec,
        out_shape=jax.ShapeDtypeStruct(grad.shape, BF16),
        compiler_params=params,
        cost_estimate=pl.CostEstimate(flops=2**31, bytes_accessed=2**22, transcendentals=0),
    )(band_start, band_count, held, other, scaled, spread)

    total, pyramid = lax.optimization_barrier((kept, pyramid))
    for x in received:
        total = total + x.astype(F32)
    total = jnp.swapaxes(total, 1, 2)
    return (jnp.swapaxes(pyramid, 3, 4), total[: out_parts // 2], total[out_parts // 2 :])


def solution(mesh):
    in_specs = (
        P(None, "rows", None, None),
        P(),
        P(),
        P("rows"),
        P("rows"),
        P("rows", None, "band", None, None),
    )
    out_specs = (
        P("rows", None, "band", None, None),
        P("rows", None, "band"),
        P("rows", None, "band"),
    )
    return jax.shard_map(shards, mesh=mesh, in_specs=in_specs, out_specs=out_specs, check_vma=False)
```

```python
import math

import jax
import jax.numpy as jnp
import numpy as np
from jax import lax
from jax.experimental import pallas as pl
from jax.experimental.pallas import tpu as pltpu
from jax.sharding import PartitionSpec as P

LEVELS = 4
BAND_REACH = 4
F32 = jnp.float32
BF16 = jnp.bfloat16
VMEM_LIMIT = 28 * 1024 * 1024
NN = (((1,), (0,)), ((), ()))
NT = (((1,), (1,)), ((), ()))
TN = (((0,), (0,)), ((), ()))


def product(a, b, dims=NN):
    return lax.dot_general(a, b, dims, preferred_element_type=F32)


def halves(x):
    high = x.astype(BF16)
    return high, (x - high.astype(F32)).astype(BF16)


def spread_matrix(pixels):
    parts = []
    for level in range(1, LEVELS):
        group = 2**level
        parts.append(np.repeat(np.eye(pixels // group, dtype=np.float32), group, axis=1) / group)
    return np.concatenate(parts, axis=0).astype(jnp.bfloat16)


def column_picker(columns):
    half = columns // 2
    taps = [
        (
            lax.broadcasted_iota(jnp.int32, (columns, half), 0)
            == 2 * lax.broadcasted_iota(jnp.int32, (columns, half), 1) + (dx - 1)
        )
        for dx in range(3)
    ]
    return jnp.concatenate([jnp.where(tap, 1.0, 0.0).astype(BF16) for tap in taps], axis=1)


def gathered(picked, rows, half):
    return jnp.concatenate(
        [
            jnp.concatenate([picked(frame, row)[:, dx * half : (dx + 1) * half] for frame in range(2)], axis=1)
            for row in rows
            for dx in range(3)
        ],
        axis=0,
    )


def stacked_weight(weight_ref, taps):
    return jnp.concatenate([weight_ref[dy, dx] for dy in taps for dx in range(3)], axis=0)


def picker_kernel(picker_ref):
    picker_ref[...] = column_picker(picker_ref.shape[0])


def local_rows_kernel(picker_ref, frames_ref, weight_ref, lower_ref, partial_ref, pick_ref):
    _, rows, channels, columns = frames_ref.shape
    half = columns // 2
    flat = frames_ref[...].reshape(2 * rows * channels, columns)
    pick_ref[...] = product(flat, picker_ref[...]).astype(BF16).reshape(pick_ref.shape)

    def picked(frame, row):
        return pick_ref[frame, row]

    lower = product(stacked_weight(weight_ref, range(3)), gathered(picked, (1, 2, 3), half), TN)
    lower_ref[...] = jnp.maximum(lower, 0.0).astype(BF16)
    partial_ref[...] = product(stacked_weight(weight_ref, (1, 2)), gathered(picked, (0, 1), half), TN)


def step_table(band):
    even = [(4, 0), (2, 0), (2, 1), (4, 1)]
    odd = [(1, 1), (1, 0), (3, 0), (3, 1)]
    table = [even, odd]
    return [table[p % len(table)] for p in range(band)]


SPLIT_BLOCKS = (0,)
SPLIT_TERMS = (2, 3)


def pixel_halves(block):
    width = block.shape[1] // 2
    return block[:, :width], block[:, width:]


def own_half(block, swapped=False):
    first, second = pixel_halves(block)
    return jnp.where((lax.div(lax.axis_index("band"), 2) == 0) != swapped, first, second)


def joined(mine, others):
    is_first = lax.div(lax.axis_index("band"), 2) == 0
    return jnp.concatenate([jnp.where(is_first, mine, others), jnp.where(is_first, others, mine)], axis=1)


def held_class(band, start_ref, count_ref, table, slots):
    place = lax.axis_index("band")
    core = lax.rem(place, 2)
    start = start_ref[0]
    swap = lax.rem(start + 2 * BAND_REACH, 2)
    slot_of = [j * band + place - core + lax.rem(core + swap, 2) for j in range(slots)]
    row = lax.axis_index("rows")
    steps = []
    for choices in zip(*table):
        step = 0
        for p, (distance, turn) in enumerate(choices):
            lower = lax.rem(lax.div(row, distance), 2) == turn
            step = jnp.where(place == p, jnp.where(lower, distance, -distance), step)
        steps.append(step)
    return swap == 0, [start + k for k in slot_of], [k < count_ref[0] for k in slot_of], steps


def target_kernel(
    band, table, factor, start_ref, count_ref, rim_ref, weight_ref, lower_ref, partial_ref, picker_ref,
    grad_ref, other_ref, spread_ref, target_ref, source_ref, own_ref, terms_ref, *refs
):
    message_refs, tile_ref = refs[:-1], refs[-1]
    half = lower_ref.shape[1] // 2
    mid = lower_ref.shape[0]
    channels = rim_ref.shape[2]
    slots = tile_ref.shape[0]
    pick = product(rim_ref[...].reshape(2 * channels, 2 * half), picker_ref[...]).astype(BF16)

    def picked(frame, row):
        return pick[frame * channels : (frame + 1) * channels]

    upper = product(stacked_weight(weight_ref, (0,)), gathered(picked, (0,), half), TN) + partial_ref[...]
    upper = jnp.maximum(upper, 0.0).astype(BF16)
    source = jnp.concatenate([upper[:, :half], lower_ref[:, :half]], axis=1)
    target = jnp.concatenate([upper[:, half:], lower_ref[:, half:]], axis=1)
    source_ref[...] = source
    same, held, active, steps = held_class(band, start_ref, count_ref, table, slots)

    def term(slot, block_ref):
        entries = product(source, block_ref[0, slot, 0], NT)
        pixels = tile_ref.shape[2]
        both = product(jnp.concatenate(halves(entries[:, pixels:]), axis=0), spread_ref[...])
        tile_ref[slot] = (entries[:, :pixels] + both[:mid] + both[mid:]).astype(BF16)

    for slot in range(slots):
        pl.when(jnp.logical_and(active[slot], same))(lambda: term(slot, grad_ref))
        pl.when(jnp.logical_and(active[slot], jnp.logical_not(same)))(lambda: term(slot, other_ref))

    def chosen(offset):
        out = jnp.zeros(tile_ref.shape[1:], BF16)
        for slot in range(slots):
            out = jnp.where(jnp.logical_and(active[slot], held[slot] == offset), tile_ref[slot], out)
        return out

    target_ref[...] = target
    own_ref[...] = chosen(0)
    for i, (step, message_ref) in enumerate(zip(steps, message_refs)):
        blocks = [own_half(target)] if i in SPLIT_BLOCKS else pixel_halves(target)
        tile = chosen(step)
        if i in SPLIT_TERMS:
            for j, part in enumerate(pixel_halves(tile)):
                terms_ref[SPLIT_TERMS.index(i), j] = part
        else:
            blocks = [*blocks, *pixel_halves(tile)]
        for j, part in enumerate(blocks):
            message_ref[j] = part


def gradient_kernel(
    band, table, factor, start_ref, count_ref, grad_ref, other_ref, spread_ref, proj_ref, target_ref, own_ref, *refs
):
    arrived, others, (held_ref, kept_ref, *sent_refs, sum_ref, out_ref) = (
        refs[: len(table[0])],
        refs[len(table[0]) : len(table[0]) + len(SPLIT_BLOCKS)],
        refs[len(table[0]) + len(SPLIT_BLOCKS) :],
    )
    slots, mid, pixels = held_ref.shape
    same, held, active, steps = held_class(band, start_ref, count_ref, table, slots)
    sum_ref[...] = jnp.zeros(sum_ref.shape, F32)

    def add(slot, block_ref):
        block = held_ref[slot]
        pooled = halves(product(block, spread_ref[...], NT))
        both = product(jnp.concatenate(pooled, axis=0), block_ref[0, slot, 0, pixels:, :])
        sum_ref[...] += product(block, block_ref[0, slot, 0, :pixels, :]) + (both[:mid] + both[mid:])

    for slot in range(slots):
        block = target_ref[...]
        for i, (step, part) in enumerate(zip(steps, arrived)):
            if i in SPLIT_BLOCKS:
                came = joined(part[0], others[SPLIT_BLOCKS.index(i)][...])
            else:
                came = jnp.concatenate([part[0], part[1]], axis=1)
            block = jnp.where(held[slot] == step, came, block)
        held_ref[slot] = block
        pl.when(jnp.logical_and(active[slot], same))(lambda: add(slot, grad_ref))
        pl.when(jnp.logical_and(active[slot], jnp.logical_not(same)))(lambda: add(slot, other_ref))

    total = own_ref[...].astype(F32)
    nothing = jnp.zeros((mid, pixels // 2), BF16)
    for i, part in enumerate(arrived):
        last = part.shape[0] - 1
        if i in SPLIT_TERMS:
            came = joined(part[last], nothing)
        else:
            came = jnp.concatenate([part[last - 1], part[last]], axis=1)
        total = total + came.astype(F32)
    high, low = halves(jnp.concatenate([sum_ref[...], total], axis=1))
    out_ref[...] = (product(proj_ref[...], high, TN) + product(proj_ref[...], low, TN)) * factor
    parts, share, width = kept_ref.shape
    place = lax.axis_index("band")
    for k in range(band):
        first = pl.multiple_of(jnp.bitwise_xor(place, k) * share, share)
        for part in range(parts):
            out = out_ref[pl.ds(first, share), part * width : (part + 1) * width]
            if k == 0:
                kept_ref[part] = out
            else:
                sent_refs[k - 1][part] = out.astype(BF16)


def pyramid_kernel(
    band, factor, start_ref, count_ref, held_ref, other_ref, source_ref, proj_ref, spread_ref, pyramid_ref, scaled_ref
):
    mid = source_ref.shape[0]
    slot = pl.program_id(0)
    active = slot * band + lax.axis_index("band") < count_ref[0]
    same = lax.rem(start_ref[0] + 2 * BAND_REACH, 2) == 0

    @pl.when(slot == 0)
    def _():
        gram = product(proj_ref[...], proj_ref[...], NT)
        both = product(jnp.concatenate(halves(gram), axis=0), source_ref[...])
        high, low = halves((both[:mid] + both[mid:]) * factor)
        scaled_ref[:mid, :] = high
        scaled_ref[mid : 2 * mid, :] = low
        scaled_ref[2 * mid :, :] = high

    @pl.when(active)
    def _():
        target = jnp.where(same, held_ref[0], other_ref[0])
        pixels = target.shape[1]
        finest = product(jnp.concatenate([target, target], axis=0), scaled_ref[: 2 * mid, :], TN)
        pyramid_ref[0, 0, 0, :pixels, :] = finest.astype(BF16)
        high, low = halves(product(spread_ref[...], target, NT))
        coarser = product(jnp.concatenate([high, high, low], axis=1), scaled_ref[...])
        pyramid_ref[0, 0, 0, pixels:, :] = coarser.astype(BF16)

    @pl.when(jnp.logical_not(active))
    def _():
        pyramid_ref[0, 0, 0] = jnp.zeros(pyramid_ref.shape[3:], BF16)


def shards(frames, conv_weight, proj_weight, band_start, band_count, pyramid_grad):
    band = lax.axis_size("band")
    row_blocks = lax.axis_size("rows")
    mid, channels = proj_weight.shape
    share = channels // band
    factor = 1.0 / math.sqrt(channels)
    frames = jnp.swapaxes(frames, 2, 3)
    grad = jnp.swapaxes(pyramid_grad, 3, 4)
    slots = grad.shape[1]
    entries, pixels = grad.shape[3:]
    columns = frames.shape[3]
    half = columns // 2
    params = pltpu.CompilerParams(vmem_limit_bytes=VMEM_LIMIT)
    smem = pl.BlockSpec(memory_space=pltpu.SMEM)
    vmem = pl.BlockSpec(memory_space=pltpu.VMEM)
    spread = jnp.asarray(spread_matrix(pixels))

    table = step_table(band)
    steps = len(table[0])

    def along_rows(x, step):
        pairs = []
        for p in range(band):
            distance, turn = table[p][step]
            for row in range(row_blocks - distance):
                if row // distance % 2 == turn:
                    pairs.append((row * band + p, (row + distance) * band + p))
                    pairs.append(((row + distance) * band + p, row * band + p))
        return lax.ppermute(x, ("rows", "band"), pairs)

    def across(x, k):
        return lax.ppermute(x, "band", [(p, p ^ k) for p in range(band)])

    rim = lax.ppermute(frames[:, -1:], "rows", [(i, i + 1) for i in range(row_blocks - 1)])
    other_grad = across(grad, 1)
    picker = pl.pallas_call(
        picker_kernel,
        out_shape=jax.ShapeDtypeStruct((columns, 3 * half), BF16),
        compiler_params=params,
        cost_estimate=pl.CostEstimate(flops=2**33, bytes_accessed=2**21, transcendentals=0),
    )()
    lower, partial = pl.pallas_call(
        local_rows_kernel,
        out_shape=(
            jax.ShapeDtypeStruct((mid, columns), BF16),
            jax.ShapeDtypeStruct((mid, columns), F32),
        ),
        scratch_shapes=[pltpu.VMEM(frames.shape[:3] + (3 * half,), BF16)],
        compiler_params=params,
        cost_estimate=pl.CostEstimate(flops=2**31, bytes_accessed=2**21, transcendentals=0),
    )(picker, frames, conv_weight)

    block = jax.ShapeDtypeStruct((mid, pixels), BF16)
    piece = (mid, pixels // 2)
    split_terms = jax.ShapeDtypeStruct((len(SPLIT_TERMS), 2) + piece, BF16)
    messages = [
        jax.ShapeDtypeStruct(((1 if i in SPLIT_BLOCKS else 2) + (0 if i in SPLIT_TERMS else 2),) + piece, BF16)
        for i in range(steps)
    ]
    target, source, own_term, terms, *messages = pl.pallas_call(
        lambda *refs: target_kernel(band, table, factor, *refs),
        in_specs=[smem] * 2 + [vmem] * 8,
        out_shape=(block, block, block, split_terms, *messages),
        scratch_shapes=[pltpu.VMEM((slots, mid, pixels), BF16)],
        compiler_params=params,
        cost_estimate=pl.CostEstimate(flops=2**31, bytes_accessed=2**22, transcendentals=0),
    )(band_start, band_count, rim, conv_weight, lower, partial, picker, grad, other_grad, spread)

    first = lax.axis_index("band") // 2 == 0
    others = across(jnp.where(first, terms[:, 1], terms[:, 0]), 2)
    terms = jnp.where(first, terms[:, 0], terms[:, 1])
    for j, i in enumerate(SPLIT_TERMS):
        messages[i] = jnp.concatenate([messages[i], terms[j : j + 1] + others[j : j + 1]])
    arrived = [along_rows(messages[i], i) for i in range(steps)]
    other_blocks = [across(arrived[i][0], 2) for i in SPLIT_BLOCKS]

    out_parts = 2 * pixels // half
    part = (out_parts, share, half)
    held, kept, *sent = pl.pallas_call(
        lambda *refs: gradient_kernel(band, table, factor, *refs),
        in_specs=[smem] * 2 + [vmem] * (6 + steps + len(SPLIT_BLOCKS)),
        out_shape=(jax.ShapeDtypeStruct((slots, mid, pixels), BF16), jax.ShapeDtypeStruct(part, F32))
        + (jax.ShapeDtypeStruct(part, BF16),) * (band - 1),
        scratch_shapes=[pltpu.VMEM((mid, pixels), F32), pltpu.VMEM((channels, 2 * pixels), F32)],
        compiler_params=params,
        cost_estimate=pl.CostEstimate(flops=2**31, bytes_accessed=2**22, transcendentals=0),
    )(band_start, band_count, grad, other_grad, spread, proj_weight, target, own_term, *arrived, *other_blocks)

    received = [across(sent[k - 1], k) for k in reversed(range(1, band))]
    other = across(held, 1)

    def whole(shape):
        return pl.BlockSpec(shape, lambda j: (0,) * len(shape))

    target_spec = pl.BlockSpec((1, mid, pixels), lambda j: (j, 0, 0))
    grad_spec = pl.BlockSpec((1, 1, 1, entries, pixels), lambda j: (0, j, 0, 0, 0))
    pyramid = pl.pallas_call(
        lambda *refs: pyramid_kernel(band, factor, *refs),
        grid=(slots,),
        in_specs=[smem, smem, target_spec, target_spec, whole((mid, pixels)), whole((mid, channels))]
        + [whole(spread.shape)],
        out_specs=grad_spec,
        out_shape=jax.ShapeDtypeStruct(grad.shape, BF16),
        scratch_shapes=[pltpu.VMEM((3 * mid, pixels), BF16)],
        compiler_params=params,
        cost_estimate=pl.CostEstimate(flops=2**31, bytes_accessed=2**22, transcendentals=0),
    )(band_start, band_count, held, other, source, proj_weight, spread)

    total, pyramid = lax.optimization_barrier((kept, pyramid))
    for x in received:
        total = total + x.astype(F32)
    total = jnp.swapaxes(total, 1, 2)
    return (jnp.swapaxes(pyramid, 3, 4), total[: out_parts // 2], total[out_parts // 2 :])


def solution(mesh):
    in_specs = (
        P(None, "rows", None, None),
        P(),
        P(),
        P("rows"),
        P("rows"),
        P("rows", None, "band", None, None),
    )
    out_specs = (
        P("rows", None, "band", None, None),
        P("rows", None, "band"),
        P("rows", None, "band"),
    )
    return jax.shard_map(shards, mesh=mesh, in_specs=in_specs, out_specs=out_specs, check_vma=False)
```

```python
import math

import jax
import jax.numpy as jnp
import numpy as np
from jax import lax
from jax.experimental import pallas as pl
from jax.experimental.pallas import tpu as pltpu
from jax.sharding import PartitionSpec as P

LEVELS = 4
BAND_REACH = 4
F32 = jnp.float32
BF16 = jnp.bfloat16
VMEM_LIMIT = 28 * 1024 * 1024
NN = (((1,), (0,)), ((), ()))
NT = (((1,), (1,)), ((), ()))
TN = (((0,), (0,)), ((), ()))


def product(a, b, dims=NN):
    return lax.dot_general(a, b, dims, preferred_element_type=F32)


def halves(x):
    high = x.astype(BF16)
    return high, (x - high.astype(F32)).astype(BF16)


def spread_matrix(pixels):
    parts = []
    for level in range(1, LEVELS):
        group = 2**level
        parts.append(np.repeat(np.eye(pixels // group, dtype=np.float32), group, axis=1) / group)
    return np.concatenate(parts, axis=0).astype(jnp.bfloat16)


def column_picker(columns):
    half = columns // 2
    taps = [
        (
            lax.broadcasted_iota(jnp.int32, (columns, half), 0)
            == 2 * lax.broadcasted_iota(jnp.int32, (columns, half), 1) + (dx - 1)
        )
        for dx in range(3)
    ]
    return jnp.concatenate([jnp.where(tap, 1.0, 0.0).astype(BF16) for tap in taps], axis=1)


def gathered(picked, rows, half):
    return jnp.concatenate(
        [
            jnp.concatenate([picked(frame, row)[:, dx * half : (dx + 1) * half] for frame in range(2)], axis=1)
            for row in rows
            for dx in range(3)
        ],
        axis=0,
    )


def stacked_weight(weight_ref, taps):
    return jnp.concatenate([weight_ref[dy, dx] for dy in taps for dx in range(3)], axis=0)


def picker_kernel(picker_ref):
    picker_ref[...] = column_picker(picker_ref.shape[0])


def local_rows_kernel(picker_ref, frames_ref, weight_ref, lower_ref, partial_ref, pick_ref):
    _, rows, channels, columns = frames_ref.shape
    half = columns // 2
    flat = frames_ref[...].reshape(2 * rows * channels, columns)
    pick_ref[...] = product(flat, picker_ref[...]).astype(BF16).reshape(pick_ref.shape)

    def picked(frame, row):
        return pick_ref[frame, row]

    lower = product(stacked_weight(weight_ref, range(3)), gathered(picked, (1, 2, 3), half), TN)
    lower_ref[...] = jnp.maximum(lower, 0.0).astype(BF16)
    partial_ref[...] = product(stacked_weight(weight_ref, (1, 2)), gathered(picked, (0, 1), half), TN)


def step_table(band):
    even = [(4, 0), (2, 0), (2, 1), (4, 1)]
    odd = [(1, 0), (1, 1), (3, 0), (3, 1)]
    table = [even, odd]
    return [table[p % len(table)] for p in range(band)]


SPLIT_BLOCKS = (0,)
SPLIT_TERMS = (2, 3)


def pixel_halves(block):
    width = block.shape[1] // 2
    return block[:, :width], block[:, width:]


def own_half(block, swapped=False):
    first, second = pixel_halves(block)
    return jnp.where((lax.div(lax.axis_index("band"), 2) == 0) != swapped, first, second)


def joined(mine, others):
    is_first = lax.div(lax.axis_index("band"), 2) == 0
    return jnp.concatenate([jnp.where(is_first, mine, others), jnp.where(is_first, others, mine)], axis=1)


def held_class(band, start_ref, count_ref, table, slots):
    place = lax.axis_index("band")
    core = lax.rem(place, 2)
    start = start_ref[0]
    swap = lax.rem(start + 2 * BAND_REACH, 2)
    slot_of = [j * band + place - core + lax.rem(core + swap, 2) for j in range(slots)]
    row = lax.axis_index("rows")
    steps = []
    for choices in zip(*table):
        step = 0
        for p, (distance, turn) in enumerate(choices):
            lower = lax.rem(lax.div(row, distance), 2) == turn
            step = jnp.where(place == p, jnp.where(lower, distance, -distance), step)
        steps.append(step)
    return swap == 0, [start + k for k in slot_of], [k < count_ref[0] for k in slot_of], steps


def target_kernel(
    band, table, factor, start_ref, count_ref, rim_ref, weight_ref, lower_ref, partial_ref, picker_ref,
    grad_ref, other_ref, spread_ref, target_ref, source_ref, own_ref, terms_ref, *refs
):
    message_refs, tile_ref = refs[:-1], refs[-1]
    half = lower_ref.shape[1] // 2
    mid = lower_ref.shape[0]
    channels = rim_ref.shape[2]
    slots = tile_ref.shape[0]
    pick = product(rim_ref[...].reshape(2 * channels, 2 * half), picker_ref[...]).astype(BF16)

    def picked(frame, row):
        return pick[frame * channels : (frame + 1) * channels]

    upper = product(stacked_weight(weight_ref, (0,)), gathered(picked, (0,), half), TN) + partial_ref[...]
    upper = jnp.maximum(upper, 0.0).astype(BF16)
    source = jnp.concatenate([upper[:, :half], lower_ref[:, :half]], axis=1)
    target = jnp.concatenate([upper[:, half:], lower_ref[:, half:]], axis=1)
    source_ref[...] = source
    same, held, active, steps = held_class(band, start_ref, count_ref, table, slots)

    def term(slot, block_ref):
        entries = product(source, block_ref[0, slot, 0], NT)
        pixels = tile_ref.shape[2]
        both = product(jnp.concatenate(halves(entries[:, pixels:]), axis=0), spread_ref[...])
        tile_ref[slot] = (entries[:, :pixels] + both[:mid] + both[mid:]).astype(BF16)

    for slot in range(slots):
        pl.when(jnp.logical_and(active[slot], same))(lambda: term(slot, grad_ref))
        pl.when(jnp.logical_and(active[slot], jnp.logical_not(same)))(lambda: term(slot, other_ref))

    def chosen(offset):
        out = jnp.zeros(tile_ref.shape[1:], BF16)
        for slot in range(slots):
            out = jnp.where(jnp.logical_and(active[slot], held[slot] == offset), tile_ref[slot], out)
        return out

    target_ref[...] = target
    own_ref[...] = chosen(0)
    for i, step in enumerate(steps):
        tile = chosen(step)
        if i in SPLIT_TERMS:
            for j, part in enumerate(pixel_halves(tile)):
                terms_ref[SPLIT_TERMS.index(i), j] = part
        else:
            blocks = [own_half(target)] if i in SPLIT_BLOCKS else []
            for j, part in enumerate([*blocks, *pixel_halves(tile)]):
                message_refs[i][j] = part


def pieces_kernel(target_ref, pieces_ref):
    for j, part in enumerate(pixel_halves(target_ref[...])):
        pieces_ref[j] = part


def gradient_kernel(
    band, table, factor, start_ref, count_ref, grad_ref, other_ref, spread_ref, proj_ref, target_ref, own_ref, *refs
):
    arrived, others, (held_ref, kept_ref, *sent_refs, sum_ref, out_ref) = (
        refs[: len(table[0])],
        refs[len(table[0]) : len(table[0]) + len(SPLIT_BLOCKS)],
        refs[len(table[0]) + len(SPLIT_BLOCKS) :],
    )
    slots, mid, pixels = held_ref.shape
    same, held, active, steps = held_class(band, start_ref, count_ref, table, slots)
    sum_ref[...] = jnp.zeros(sum_ref.shape, F32)

    def add(slot, block_ref):
        block = held_ref[slot]
        pooled = halves(product(block, spread_ref[...], NT))
        both = product(jnp.concatenate(pooled, axis=0), block_ref[0, slot, 0, pixels:, :])
        sum_ref[...] += product(block, block_ref[0, slot, 0, :pixels, :]) + (both[:mid] + both[mid:])

    for slot in range(slots):
        block = target_ref[...]
        for i, (step, part) in enumerate(zip(steps, arrived)):
            if i in SPLIT_BLOCKS:
                came = joined(part[0], others[SPLIT_BLOCKS.index(i)][...])
            else:
                came = jnp.concatenate([part[0], part[1]], axis=1)
            block = jnp.where(held[slot] == step, came, block)
        held_ref[slot] = block
        pl.when(jnp.logical_and(active[slot], same))(lambda: add(slot, grad_ref))
        pl.when(jnp.logical_and(active[slot], jnp.logical_not(same)))(lambda: add(slot, other_ref))

    total = own_ref[...].astype(F32)
    nothing = jnp.zeros((mid, pixels // 2), BF16)
    for i, part in enumerate(arrived):
        last = part.shape[0] - 1
        if i in SPLIT_TERMS:
            came = joined(part[last], nothing)
        else:
            came = jnp.concatenate([part[last - 1], part[last]], axis=1)
        total = total + came.astype(F32)
    high, low = halves(jnp.concatenate([sum_ref[...], total], axis=1))
    out_ref[...] = (product(proj_ref[...], high, TN) + product(proj_ref[...], low, TN)) * factor
    parts, share, width = kept_ref.shape
    place = lax.axis_index("band")
    for k in range(band):
        first = pl.multiple_of(jnp.bitwise_xor(place, k) * share, share)
        for part in range(parts):
            out = out_ref[pl.ds(first, share), part * width : (part + 1) * width]
            if k == 0:
                kept_ref[part] = out
            else:
                sent_refs[k - 1][part] = out.astype(BF16)


def pyramid_kernel(
    band, factor, start_ref, count_ref, held_ref, other_ref, source_ref, proj_ref, spread_ref, pyramid_ref, scaled_ref
):
    mid = source_ref.shape[0]
    slot = pl.program_id(0)
    active = slot * band + lax.axis_index("band") < count_ref[0]
    same = lax.rem(start_ref[0] + 2 * BAND_REACH, 2) == 0

    @pl.when(slot == 0)
    def _():
        gram = product(proj_ref[...], proj_ref[...], NT)
        both = product(jnp.concatenate(halves(gram), axis=0), source_ref[...])
        high, low = halves((both[:mid] + both[mid:]) * factor)
        scaled_ref[:mid, :] = high
        scaled_ref[mid : 2 * mid, :] = low
        scaled_ref[2 * mid :, :] = high

    @pl.when(active)
    def _():
        target = jnp.where(same, held_ref[0], other_ref[0])
        pixels = target.shape[1]
        finest = product(jnp.concatenate([target, target], axis=0), scaled_ref[: 2 * mid, :], TN)
        pyramid_ref[0, 0, 0, :pixels, :] = finest.astype(BF16)
        high, low = halves(product(spread_ref[...], target, NT))
        coarser = product(jnp.concatenate([high, high, low], axis=1), scaled_ref[...])
        pyramid_ref[0, 0, 0, pixels:, :] = coarser.astype(BF16)

    @pl.when(jnp.logical_not(active))
    def _():
        pyramid_ref[0, 0, 0] = jnp.zeros(pyramid_ref.shape[3:], BF16)


def shards(frames, conv_weight, proj_weight, band_start, band_count, pyramid_grad):
    band = lax.axis_size("band")
    row_blocks = lax.axis_size("rows")
    mid, channels = proj_weight.shape
    share = channels // band
    factor = 1.0 / math.sqrt(channels)
    frames = jnp.swapaxes(frames, 2, 3)
    grad = jnp.swapaxes(pyramid_grad, 3, 4)
    slots = grad.shape[1]
    entries, pixels = grad.shape[3:]
    columns = frames.shape[3]
    half = columns // 2
    params = pltpu.CompilerParams(vmem_limit_bytes=VMEM_LIMIT)
    smem = pl.BlockSpec(memory_space=pltpu.SMEM)
    vmem = pl.BlockSpec(memory_space=pltpu.VMEM)
    spread = jnp.asarray(spread_matrix(pixels))

    table = step_table(band)
    steps = len(table[0])

    def along_rows(x, step):
        pairs = []
        for p in range(band):
            distance, turn = table[p][step]
            for row in range(row_blocks - distance):
                if row // distance % 2 == turn:
                    pairs.append((row * band + p, (row + distance) * band + p))
                    pairs.append(((row + distance) * band + p, row * band + p))
        return lax.ppermute(x, ("rows", "band"), pairs)

    def across(x, k):
        return lax.ppermute(x, "band", [(p, p ^ k) for p in range(band)])

    rim = lax.ppermute(frames[:, -1:], "rows", [(i, i + 1) for i in range(row_blocks - 1)])
    other_grad = across(grad, 1)
    picker = pl.pallas_call(
        picker_kernel,
        out_shape=jax.ShapeDtypeStruct((columns, 3 * half), BF16),
        compiler_params=params,
        cost_estimate=pl.CostEstimate(flops=2**33, bytes_accessed=2**21, transcendentals=0),
    )()
    lower, partial = pl.pallas_call(
        local_rows_kernel,
        out_shape=(
            jax.ShapeDtypeStruct((mid, columns), BF16),
            jax.ShapeDtypeStruct((mid, columns), F32),
        ),
        scratch_shapes=[pltpu.VMEM(frames.shape[:3] + (3 * half,), BF16)],
        compiler_params=params,
        cost_estimate=pl.CostEstimate(flops=2**31, bytes_accessed=2**21, transcendentals=0),
    )(picker, frames, conv_weight)

    block = jax.ShapeDtypeStruct((mid, pixels), BF16)
    piece = (mid, pixels // 2)
    split_terms = jax.ShapeDtypeStruct((len(SPLIT_TERMS), 2) + piece, BF16)
    messages = [
        jax.ShapeDtypeStruct(((1 if i in SPLIT_BLOCKS else 0) + 2,) + piece, BF16)
        for i in range(steps)
        if i not in SPLIT_TERMS
    ]
    target, source, own_term, terms, *messages = pl.pallas_call(
        lambda *refs: target_kernel(band, table, factor, *refs),
        in_specs=[smem] * 2 + [vmem] * 8,
        out_shape=(block, block, block, split_terms, *messages),
        scratch_shapes=[pltpu.VMEM((slots, mid, pixels), BF16)],
        compiler_params=params,
        cost_estimate=pl.CostEstimate(flops=2**31, bytes_accessed=2**22, transcendentals=0),
    )(band_start, band_count, rim, conv_weight, lower, partial, picker, grad, other_grad, spread)

    first = lax.axis_index("band") // 2 == 0
    others = across(jnp.where(first, terms[:, 1], terms[:, 0]), 2)
    terms = jnp.where(first, terms[:, 0], terms[:, 1])
    pieces = pl.pallas_call(
        pieces_kernel,
        out_shape=jax.ShapeDtypeStruct((2,) + piece, BF16),
        compiler_params=params,
        cost_estimate=pl.CostEstimate(flops=2**31, bytes_accessed=2**20, transcendentals=0),
    )(target)
    for i in range(len(messages)):
        if i not in SPLIT_BLOCKS:
            messages[i] = jnp.concatenate([pieces, messages[i]])
    for j, i in enumerate(SPLIT_TERMS):
        messages.insert(i, jnp.concatenate([pieces, terms[j : j + 1] + others[j : j + 1]]))
    arrived = [along_rows(messages[i], i) for i in range(steps)]
    other_blocks = [across(arrived[i][0], 2) for i in SPLIT_BLOCKS]

    out_parts = 2 * pixels // half
    part = (out_parts, share, half)
    held, kept, *sent = pl.pallas_call(
        lambda *refs: gradient_kernel(band, table, factor, *refs),
        in_specs=[smem] * 2 + [vmem] * (6 + steps + len(SPLIT_BLOCKS)),
        out_shape=(jax.ShapeDtypeStruct((slots, mid, pixels), BF16), jax.ShapeDtypeStruct(part, F32))
        + (jax.ShapeDtypeStruct(part, BF16),) * (band - 1),
        scratch_shapes=[pltpu.VMEM((mid, pixels), F32), pltpu.VMEM((channels, 2 * pixels), F32)],
        compiler_params=params,
        cost_estimate=pl.CostEstimate(flops=2**31, bytes_accessed=2**22, transcendentals=0),
    )(band_start, band_count, grad, other_grad, spread, proj_weight, target, own_term, *arrived, *other_blocks)

    received = [across(sent[k - 1], k) for k in reversed(range(1, band))]
    other = across(held, 1)

    def whole(shape):
        return pl.BlockSpec(shape, lambda j: (0,) * len(shape))

    target_spec = pl.BlockSpec((1, mid, pixels), lambda j: (j, 0, 0))
    grad_spec = pl.BlockSpec((1, 1, 1, entries, pixels), lambda j: (0, j, 0, 0, 0))
    pyramid = pl.pallas_call(
        lambda *refs: pyramid_kernel(band, factor, *refs),
        grid=(slots,),
        in_specs=[smem, smem, target_spec, target_spec, whole((mid, pixels)), whole((mid, channels))]
        + [whole(spread.shape)],
        out_specs=grad_spec,
        out_shape=jax.ShapeDtypeStruct(grad.shape, BF16),
        scratch_shapes=[pltpu.VMEM((3 * mid, pixels), BF16)],
        compiler_params=params,
        cost_estimate=pl.CostEstimate(flops=2**31, bytes_accessed=2**22, transcendentals=0),
    )(band_start, band_count, held, other, source, proj_weight, spread)

    total, pyramid = lax.optimization_barrier((kept, pyramid))
    for x in received:
        total = total + x.astype(F32)
    total = jnp.swapaxes(total, 1, 2)
    return (jnp.swapaxes(pyramid, 3, 4), total[: out_parts // 2], total[out_parts // 2 :])


def solution(mesh):
    in_specs = (
        P(None, "rows", None, None),
        P(),
        P(),
        P("rows"),
        P("rows"),
        P("rows", None, "band", None, None),
    )
    out_specs = (
        P("rows", None, "band", None, None),
        P("rows", None, "band"),
        P("rows", None, "band"),
    )
    return jax.shard_map(shards, mesh=mesh, in_specs=in_specs, out_specs=out_specs, check_vma=False)
```

```python
import math

import jax
import jax.numpy as jnp
import numpy as np
from jax import lax
from jax.experimental import pallas as pl
from jax.experimental.pallas import tpu as pltpu
from jax.sharding import PartitionSpec as P

LEVELS = 4
BAND_REACH = 4
F32 = jnp.float32
BF16 = jnp.bfloat16
VMEM_LIMIT = 28 * 1024 * 1024
NN = (((1,), (0,)), ((), ()))
NT = (((1,), (1,)), ((), ()))
TN = (((0,), (0,)), ((), ()))


def product(a, b, dims=NN):
    return lax.dot_general(a, b, dims, preferred_element_type=F32)


def halves(x):
    high = x.astype(BF16)
    return high, (x - high.astype(F32)).astype(BF16)


def spread_matrix(pixels):
    parts = []
    for level in range(1, LEVELS):
        group = 2**level
        parts.append(np.repeat(np.eye(pixels // group, dtype=np.float32), group, axis=1) / group)
    return np.concatenate(parts, axis=0).astype(jnp.bfloat16)


def column_picker(columns):
    half = columns // 2
    taps = [
        (
            lax.broadcasted_iota(jnp.int32, (columns, half), 0)
            == 2 * lax.broadcasted_iota(jnp.int32, (columns, half), 1) + (dx - 1)
        )
        for dx in range(3)
    ]
    return jnp.concatenate([jnp.where(tap, 1.0, 0.0).astype(BF16) for tap in taps], axis=1)


def gathered(picked, rows, half):
    return jnp.concatenate(
        [
            jnp.concatenate([picked(frame, row)[:, dx * half : (dx + 1) * half] for frame in range(2)], axis=1)
            for row in rows
            for dx in range(3)
        ],
        axis=0,
    )


def stacked_weight(weight_ref, taps):
    return jnp.concatenate([weight_ref[dy, dx] for dy in taps for dx in range(3)], axis=0)


def picker_kernel(picker_ref):
    picker_ref[...] = column_picker(picker_ref.shape[0])


def local_rows_kernel(picker_ref, frames_ref, weight_ref, lower_ref, partial_ref, pick_ref):
    _, rows, channels, columns = frames_ref.shape
    half = columns // 2
    flat = frames_ref[...].reshape(2 * rows * channels, columns)
    pick_ref[...] = product(flat, picker_ref[...]).astype(BF16).reshape(pick_ref.shape)

    def picked(frame, row):
        return pick_ref[frame, row]

    lower = product(stacked_weight(weight_ref, range(3)), gathered(picked, (1, 2, 3), half), TN)
    lower_ref[...] = jnp.maximum(lower, 0.0).astype(BF16)
    partial_ref[...] = product(stacked_weight(weight_ref, (1, 2)), gathered(picked, (0, 1), half), TN)


def step_table(band):
    even = [(4, 0), (2, 0), (2, 1), (4, 1)]
    odd = [(1, 0), (1, 1), (3, 0), (3, 1)]
    table = [even, odd]
    return [table[p % len(table)] for p in range(band)]


SPLIT_BLOCKS = (0,)
SPLIT_TERMS = (2, 3)


def pixel_halves(block):
    width = block.shape[1] // 2
    return block[:, :width], block[:, width:]


def own_half(block, swapped=False):
    first, second = pixel_halves(block)
    return jnp.where((lax.div(lax.axis_index("band"), 2) == 0) != swapped, first, second)


def joined(mine, others):
    is_first = lax.div(lax.axis_index("band"), 2) == 0
    return jnp.concatenate([jnp.where(is_first, mine, others), jnp.where(is_first, others, mine)], axis=1)


def held_class(band, start_ref, count_ref, table, slots):
    place = lax.axis_index("band")
    core = lax.rem(place, 2)
    start = start_ref[0]
    swap = lax.rem(start + 2 * BAND_REACH, 2)
    slot_of = [j * band + place - core + lax.rem(core + swap, 2) for j in range(slots)]
    row = lax.axis_index("rows")
    steps = []
    for choices in zip(*table):
        step = 0
        for p, (distance, turn) in enumerate(choices):
            lower = lax.rem(lax.div(row, distance), 2) == turn
            step = jnp.where(place == p, jnp.where(lower, distance, -distance), step)
        steps.append(step)
    return swap == 0, [start + k for k in slot_of], [k < count_ref[0] for k in slot_of], steps


def target_kernel(
    band, table, factor, start_ref, count_ref, rim_ref, weight_ref, lower_ref, partial_ref, picker_ref,
    grad_ref, other_ref, spread_ref, target_ref, source_ref, own_ref, terms_ref, *refs
):
    message_refs, tile_ref = refs[:-1], refs[-1]
    half = lower_ref.shape[1] // 2
    mid = lower_ref.shape[0]
    channels = rim_ref.shape[2]
    slots = tile_ref.shape[0]
    pick = product(rim_ref[...].reshape(2 * channels, 2 * half), picker_ref[...]).astype(BF16)

    def picked(frame, row):
        return pick[frame * channels : (frame + 1) * channels]

    upper = product(stacked_weight(weight_ref, (0,)), gathered(picked, (0,), half), TN) + partial_ref[...]
    upper = jnp.maximum(upper, 0.0).astype(BF16)
    source = jnp.concatenate([upper[:, :half], lower_ref[:, :half]], axis=1)
    target = jnp.concatenate([upper[:, half:], lower_ref[:, half:]], axis=1)
    source_ref[...] = source
    same, held, active, steps = held_class(band, start_ref, count_ref, table, slots)

    def term(slot, block_ref):
        entries = product(source, block_ref[0, slot, 0], NT)
        pixels = tile_ref.shape[2]
        both = product(jnp.concatenate(halves(entries[:, pixels:]), axis=0), spread_ref[...])
        tile_ref[slot] = (entries[:, :pixels] + both[:mid] + both[mid:]).astype(BF16)

    for slot in range(slots):
        pl.when(jnp.logical_and(active[slot], same))(lambda: term(slot, grad_ref))
        pl.when(jnp.logical_and(active[slot], jnp.logical_not(same)))(lambda: term(slot, other_ref))

    def chosen(offset):
        out = jnp.zeros(tile_ref.shape[1:], BF16)
        for slot in range(slots):
            out = jnp.where(jnp.logical_and(active[slot], held[slot] == offset), tile_ref[slot], out)
        return out

    target_ref[...] = target
    own_ref[...] = chosen(0)
    for i, step in enumerate(steps):
        tile = chosen(step)
        if i in SPLIT_TERMS:
            for j, part in enumerate(pixel_halves(tile)):
                terms_ref[SPLIT_TERMS.index(i), j] = part
        else:
            blocks = [own_half(target)] if i in SPLIT_BLOCKS else []
            for j, part in enumerate([*blocks, *pixel_halves(tile)]):
                message_refs[i][j] = part


def pieces_kernel(target_ref, pieces_ref):
    for j, part in enumerate(pixel_halves(target_ref[...])):
        pieces_ref[j] = part


def gradient_kernel(
    band, table, factor, start_ref, count_ref, grad_ref, other_ref, spread_ref, proj_ref, target_ref, own_ref, *refs
):
    arrived, others, (held_ref, kept_ref, *sent_refs, sum_ref, out_ref) = (
        refs[: len(table[0])],
        refs[len(table[0]) : len(table[0]) + len(SPLIT_BLOCKS)],
        refs[len(table[0]) + len(SPLIT_BLOCKS) :],
    )
    slots, mid, pixels = held_ref.shape
    same, held, active, steps = held_class(band, start_ref, count_ref, table, slots)
    sum_ref[...] = jnp.zeros(sum_ref.shape, F32)

    def add(slot, block_ref):
        block = held_ref[slot]
        pooled = halves(product(block, spread_ref[...], NT))
        both = product(jnp.concatenate(pooled, axis=0), block_ref[0, slot, 0, pixels:, :])
        sum_ref[...] += product(block, block_ref[0, slot, 0, :pixels, :]) + (both[:mid] + both[mid:])

    for slot in range(slots):
        block = target_ref[...]
        for i, (step, part) in enumerate(zip(steps, arrived)):
            if i in SPLIT_BLOCKS:
                came = joined(part[0], others[SPLIT_BLOCKS.index(i)][...])
            else:
                came = jnp.concatenate([part[0], part[1]], axis=1)
            block = jnp.where(held[slot] == step, came, block)
        held_ref[slot] = block
        pl.when(jnp.logical_and(active[slot], same))(lambda: add(slot, grad_ref))
        pl.when(jnp.logical_and(active[slot], jnp.logical_not(same)))(lambda: add(slot, other_ref))

    total = own_ref[...].astype(F32)
    nothing = jnp.zeros((mid, pixels // 2), BF16)
    for i, part in enumerate(arrived):
        last = part.shape[0] - 1
        if i in SPLIT_TERMS:
            came = joined(part[last], nothing)
        else:
            came = jnp.concatenate([part[last - 1], part[last]], axis=1)
        total = total + came.astype(F32)
    high, low = halves(jnp.concatenate([sum_ref[...], total], axis=1))
    out_ref[...] = (product(proj_ref[...], high, TN) + product(proj_ref[...], low, TN)) * factor
    parts, share, width = kept_ref.shape
    place = lax.axis_index("band")
    for k in range(band):
        first = pl.multiple_of(jnp.bitwise_xor(place, k) * share, share)
        for part in range(parts):
            out = out_ref[pl.ds(first, share), part * width : (part + 1) * width]
            if k == 0:
                kept_ref[part] = out
            else:
                sent_refs[k - 1][part] = out.astype(BF16)


def total_kernel(kept_ref, *refs):
    received, out_refs = refs[:-2], refs[-2:]
    rows = out_refs[0].shape[0]
    for i, out_ref in enumerate(out_refs):
        total = kept_ref[i * rows : (i + 1) * rows]
        for part in received:
            total = total + part[i * rows : (i + 1) * rows].astype(F32)
        out_ref[...] = total


def pyramid_kernel(
    band, factor, start_ref, count_ref, held_ref, other_ref, source_ref, proj_ref, spread_ref, pyramid_ref, scaled_ref
):
    mid = source_ref.shape[0]
    slot = pl.program_id(0)
    active = slot * band + lax.axis_index("band") < count_ref[0]
    same = lax.rem(start_ref[0] + 2 * BAND_REACH, 2) == 0

    @pl.when(slot == 0)
    def _():
        gram = product(proj_ref[...], proj_ref[...], NT)
        both = product(jnp.concatenate(halves(gram), axis=0), source_ref[...])
        high, low = halves((both[:mid] + both[mid:]) * factor)
        scaled_ref[:mid, :] = high
        scaled_ref[mid : 2 * mid, :] = low
        scaled_ref[2 * mid :, :] = high

    @pl.when(active)
    def _():
        target = jnp.where(same, held_ref[0], other_ref[0])
        pixels = target.shape[1]
        finest = product(jnp.concatenate([target, target], axis=0), scaled_ref[: 2 * mid, :], TN)
        pyramid_ref[0, 0, 0, :pixels, :] = finest.astype(BF16)
        high, low = halves(product(spread_ref[...], target, NT))
        coarser = product(jnp.concatenate([high, high, low], axis=1), scaled_ref[...])
        pyramid_ref[0, 0, 0, pixels:, :] = coarser.astype(BF16)

    @pl.when(jnp.logical_not(active))
    def _():
        pyramid_ref[0, 0, 0] = jnp.zeros(pyramid_ref.shape[3:], BF16)


def shards(frames, conv_weight, proj_weight, band_start, band_count, pyramid_grad):
    band = lax.axis_size("band")
    row_blocks = lax.axis_size("rows")
    mid, channels = proj_weight.shape
    share = channels // band
    factor = 1.0 / math.sqrt(channels)
    frames = jnp.swapaxes(frames, 2, 3)
    grad = jnp.swapaxes(pyramid_grad, 3, 4)
    slots = grad.shape[1]
    entries, pixels = grad.shape[3:]
    columns = frames.shape[3]
    half = columns // 2
    params = pltpu.CompilerParams(vmem_limit_bytes=VMEM_LIMIT)
    smem = pl.BlockSpec(memory_space=pltpu.SMEM)
    vmem = pl.BlockSpec(memory_space=pltpu.VMEM)
    spread = jnp.asarray(spread_matrix(pixels))

    table = step_table(band)
    steps = len(table[0])

    def along_rows(x, step):
        pairs = []
        for p in range(band):
            distance, turn = table[p][step]
            for row in range(row_blocks - distance):
                if row // distance % 2 == turn:
                    pairs.append((row * band + p, (row + distance) * band + p))
                    pairs.append(((row + distance) * band + p, row * band + p))
        return lax.ppermute(x, ("rows", "band"), pairs)

    def across(x, k):
        return lax.ppermute(x, "band", [(p, p ^ k) for p in range(band)])

    rim = lax.ppermute(frames[:, -1:], "rows", [(i, i + 1) for i in range(row_blocks - 1)])
    other_grad = across(grad, 1)
    picker = pl.pallas_call(
        picker_kernel,
        out_shape=jax.ShapeDtypeStruct((columns, 3 * half), BF16),
        compiler_params=params,
        cost_estimate=pl.CostEstimate(flops=2**33, bytes_accessed=2**21, transcendentals=0),
    )()
    lower, partial = pl.pallas_call(
        local_rows_kernel,
        out_shape=(
            jax.ShapeDtypeStruct((mid, columns), BF16),
            jax.ShapeDtypeStruct((mid, columns), F32),
        ),
        scratch_shapes=[pltpu.VMEM(frames.shape[:3] + (3 * half,), BF16)],
        compiler_params=params,
        cost_estimate=pl.CostEstimate(flops=2**31, bytes_accessed=2**21, transcendentals=0),
    )(picker, frames, conv_weight)

    block = jax.ShapeDtypeStruct((mid, pixels), BF16)
    piece = (mid, pixels // 2)
    split_terms = jax.ShapeDtypeStruct((len(SPLIT_TERMS), 2) + piece, BF16)
    messages = [
        jax.ShapeDtypeStruct(((1 if i in SPLIT_BLOCKS else 0) + 2,) + piece, BF16)
        for i in range(steps)
        if i not in SPLIT_TERMS
    ]
    target, source, own_term, terms, *messages = pl.pallas_call(
        lambda *refs: target_kernel(band, table, factor, *refs),
        in_specs=[smem] * 2 + [vmem] * 8,
        out_shape=(block, block, block, split_terms, *messages),
        scratch_shapes=[pltpu.VMEM((slots, mid, pixels), BF16)],
        compiler_params=params,
        cost_estimate=pl.CostEstimate(flops=2**31, bytes_accessed=2**22, transcendentals=0),
    )(band_start, band_count, rim, conv_weight, lower, partial, picker, grad, other_grad, spread)

    first = lax.axis_index("band") // 2 == 0
    others = across(jnp.where(first, terms[:, 1], terms[:, 0]), 2)
    terms = jnp.where(first, terms[:, 0], terms[:, 1])
    pieces = pl.pallas_call(
        pieces_kernel,
        out_shape=jax.ShapeDtypeStruct((2,) + piece, BF16),
        compiler_params=params,
        cost_estimate=pl.CostEstimate(flops=2**31, bytes_accessed=2**20, transcendentals=0),
    )(target)
    for i in range(len(messages)):
        if i not in SPLIT_BLOCKS:
            messages[i] = jnp.concatenate([pieces, messages[i]])
    for j, i in enumerate(SPLIT_TERMS):
        messages.insert(i, jnp.concatenate([pieces, terms[j : j + 1] + others[j : j + 1]]))
    arrived = [along_rows(messages[i], i) for i in range(steps)]
    other_blocks = [across(arrived[i][0], 2) for i in SPLIT_BLOCKS]

    out_parts = 2 * pixels // half
    part = (out_parts, share, half)
    held, kept, *sent = pl.pallas_call(
        lambda *refs: gradient_kernel(band, table, factor, *refs),
        in_specs=[smem] * 2 + [vmem] * (6 + steps + len(SPLIT_BLOCKS)),
        out_shape=(jax.ShapeDtypeStruct((slots, mid, pixels), BF16), jax.ShapeDtypeStruct(part, F32))
        + (jax.ShapeDtypeStruct(part, BF16),) * (band - 1),
        scratch_shapes=[pltpu.VMEM((mid, pixels), F32), pltpu.VMEM((channels, 2 * pixels), F32)],
        compiler_params=params,
        cost_estimate=pl.CostEstimate(flops=2**31, bytes_accessed=2**22, transcendentals=0),
    )(band_start, band_count, grad, other_grad, spread, proj_weight, target, own_term, *arrived, *other_blocks)

    received = [across(sent[k - 1], k) for k in reversed(range(1, band))]
    other = across(held, 1)

    def whole(shape):
        return pl.BlockSpec(shape, lambda j: (0,) * len(shape))

    target_spec = pl.BlockSpec((1, mid, pixels), lambda j: (j, 0, 0))
    grad_spec = pl.BlockSpec((1, 1, 1, entries, pixels), lambda j: (0, j, 0, 0, 0))
    pyramid = pl.pallas_call(
        lambda *refs: pyramid_kernel(band, factor, *refs),
        grid=(slots,),
        in_specs=[smem, smem, target_spec, target_spec, whole((mid, pixels)), whole((mid, channels))]
        + [whole(spread.shape)],
        out_specs=grad_spec,
        out_shape=jax.ShapeDtypeStruct(grad.shape, BF16),
        scratch_shapes=[pltpu.VMEM((3 * mid, pixels), BF16)],
        compiler_params=params,
        cost_estimate=pl.CostEstimate(flops=2**31, bytes_accessed=2**22, transcendentals=0),
    )(band_start, band_count, held, other, source, proj_weight, spread)

    kept, pyramid = lax.optimization_barrier((kept, pyramid))
    half_part = jax.ShapeDtypeStruct((out_parts // 2, share, half), F32)
    source_grad, target_grad = pl.pallas_call(
        total_kernel,
        out_shape=(half_part, half_part),
        compiler_params=params,
    )(kept, *received)
    return (jnp.swapaxes(pyramid, 3, 4), jnp.swapaxes(source_grad, 1, 2), jnp.swapaxes(target_grad, 1, 2))


def solution(mesh):
    in_specs = (
        P(None, "rows", None, None),
        P(),
        P(),
        P("rows"),
        P("rows"),
        P("rows", None, "band", None, None),
    )
    out_specs = (
        P("rows", None, "band", None, None),
        P("rows", None, "band"),
        P("rows", None, "band"),
    )
    return jax.shard_map(shards, mesh=mesh, in_specs=in_specs, out_specs=out_specs, check_vma=False)
```

```python
import math

import jax
import jax.numpy as jnp
import numpy as np
from jax import lax
from jax.experimental import pallas as pl
from jax.experimental.pallas import tpu as pltpu
from jax.sharding import PartitionSpec as P

LEVELS = 4
BAND_REACH = 4
F32 = jnp.float32
BF16 = jnp.bfloat16
VMEM_LIMIT = 28 * 1024 * 1024
NN = (((1,), (0,)), ((), ()))
NT = (((1,), (1,)), ((), ()))
TN = (((0,), (0,)), ((), ()))


def product(a, b, dims=NN):
    return lax.dot_general(a, b, dims, preferred_element_type=F32)


def halves(x):
    high = x.astype(BF16)
    return high, (x - high.astype(F32)).astype(BF16)


def spread_matrix(pixels):
    parts = []
    for level in range(1, LEVELS):
        group = 2**level
        parts.append(np.repeat(np.eye(pixels // group, dtype=np.float32), group, axis=1) / group)
    return np.concatenate(parts, axis=0).astype(jnp.bfloat16)


def column_picker(columns):
    half = columns // 2
    taps = [
        (
            lax.broadcasted_iota(jnp.int32, (columns, half), 0)
            == 2 * lax.broadcasted_iota(jnp.int32, (columns, half), 1) + (dx - 1)
        )
        for dx in range(3)
    ]
    return jnp.concatenate([jnp.where(tap, 1.0, 0.0).astype(BF16) for tap in taps], axis=1)


def gathered(picked, rows, half):
    return jnp.concatenate(
        [
            jnp.concatenate([picked(frame, row)[:, dx * half : (dx + 1) * half] for frame in range(2)], axis=1)
            for row in rows
            for dx in range(3)
        ],
        axis=0,
    )


def stacked_weight(weight_ref, taps):
    return jnp.concatenate([weight_ref[dy, dx] for dy in taps for dx in range(3)], axis=0)


def picker_kernel(picker_ref):
    picker_ref[...] = column_picker(picker_ref.shape[0])


def local_rows_kernel(picker_ref, frames_ref, weight_ref, lower_ref, partial_ref, pick_ref):
    _, rows, channels, columns = frames_ref.shape
    half = columns // 2
    flat = frames_ref[...].reshape(2 * rows * channels, columns)
    pick_ref[...] = product(flat, picker_ref[...]).astype(BF16).reshape(pick_ref.shape)

    def picked(frame, row):
        return pick_ref[frame, row]

    lower = product(stacked_weight(weight_ref, range(3)), gathered(picked, (1, 2, 3), half), TN)
    lower_ref[...] = jnp.maximum(lower, 0.0).astype(BF16)
    partial_ref[...] = product(stacked_weight(weight_ref, (1, 2)), gathered(picked, (0, 1), half), TN)


def step_table(band):
    even = [(4, 0), (2, 0), (2, 1), (4, 1)]
    odd = [(1, 0), (1, 1), (3, 0), (3, 1)]
    table = [even, odd]
    return [table[p % len(table)] for p in range(band)]


SPLIT_BLOCKS = (0,)
SPLIT_TERMS = (2, 3)


def pixel_halves(block):
    width = block.shape[1] // 2
    return block[:, :width], block[:, width:]


def own_half(block, swapped=False):
    first, second = pixel_halves(block)
    return jnp.where((lax.div(lax.axis_index("band"), 2) == 0) != swapped, first, second)


def joined(mine, others):
    is_first = lax.div(lax.axis_index("band"), 2) == 0
    return jnp.concatenate([jnp.where(is_first, mine, others), jnp.where(is_first, others, mine)], axis=1)


def held_class(band, start_ref, count_ref, table, slots):
    place = lax.axis_index("band")
    core = lax.rem(place, 2)
    start = start_ref[0]
    swap = lax.rem(start + 2 * BAND_REACH, 2)
    slot_of = [j * band + place - core + lax.rem(core + swap, 2) for j in range(slots)]
    row = lax.axis_index("rows")
    steps = []
    for choices in zip(*table):
        step = 0
        for p, (distance, turn) in enumerate(choices):
            lower = lax.rem(lax.div(row, distance), 2) == turn
            step = jnp.where(place == p, jnp.where(lower, distance, -distance), step)
        steps.append(step)
    return swap == 0, [start + k for k in slot_of], [k < count_ref[0] for k in slot_of], steps


def target_kernel(
    band, table, factor, start_ref, count_ref, rim_ref, weight_ref, lower_ref, partial_ref, picker_ref,
    grad_ref, other_ref, spread_ref, target_ref, source_ref, own_ref, terms_ref, *refs
):
    message_refs, tile_ref = refs[:-1], refs[-1]
    half = lower_ref.shape[1] // 2
    mid = lower_ref.shape[0]
    channels = rim_ref.shape[2]
    slots = tile_ref.shape[0]
    pick = product(rim_ref[...].reshape(2 * channels, 2 * half), picker_ref[...]).astype(BF16)

    def picked(frame, row):
        return pick[frame * channels : (frame + 1) * channels]

    upper = product(stacked_weight(weight_ref, (0,)), gathered(picked, (0,), half), TN) + partial_ref[...]
    upper = jnp.maximum(upper, 0.0).astype(BF16)
    source = jnp.concatenate([upper[:, :half], lower_ref[:, :half]], axis=1)
    target = jnp.concatenate([upper[:, half:], lower_ref[:, half:]], axis=1)
    source_ref[...] = source
    same, held, active, steps = held_class(band, start_ref, count_ref, table, slots)

    def term(slot, block_ref):
        entries = product(source, block_ref[0, slot, 0], NT)
        pixels = tile_ref.shape[2]
        both = product(jnp.concatenate(halves(entries[:, pixels:]), axis=0), spread_ref[...])
        tile_ref[slot] = (entries[:, :pixels] + both[:mid] + both[mid:]).astype(BF16)

    for slot in range(slots):
        pl.when(jnp.logical_and(active[slot], same))(lambda: term(slot, grad_ref))
        pl.when(jnp.logical_and(active[slot], jnp.logical_not(same)))(lambda: term(slot, other_ref))

    def chosen(offset):
        out = jnp.zeros(tile_ref.shape[1:], BF16)
        for slot in range(slots):
            out = jnp.where(jnp.logical_and(active[slot], held[slot] == offset), tile_ref[slot], out)
        return out

    target_ref[...] = target
    own_ref[...] = chosen(0)
    for i, step in enumerate(steps):
        tile = chosen(step)
        if i in SPLIT_TERMS:
            for j, part in enumerate(pixel_halves(tile)):
                terms_ref[SPLIT_TERMS.index(i), j] = part
        else:
            blocks = [own_half(target)] if i in SPLIT_BLOCKS else []
            for j, part in enumerate([*blocks, *pixel_halves(tile)]):
                message_refs[i][j] = part


def pieces_kernel(target_ref, pieces_ref):
    for j, part in enumerate(pixel_halves(target_ref[...])):
        pieces_ref[j] = part


def gradient_kernel(
    band, table, factor, start_ref, count_ref, grad_ref, other_ref, spread_ref, proj_ref, target_ref, own_ref, *refs
):
    arrived, others, (held_ref, kept_ref, *sent_refs, sum_ref, out_ref) = (
        refs[: len(table[0])],
        refs[len(table[0]) : len(table[0]) + len(SPLIT_BLOCKS)],
        refs[len(table[0]) + len(SPLIT_BLOCKS) :],
    )
    slots, mid, pixels = held_ref.shape
    same, held, active, steps = held_class(band, start_ref, count_ref, table, slots)
    sum_ref[...] = jnp.zeros(sum_ref.shape, F32)

    def add(slot, block_ref):
        block = held_ref[slot]
        pooled = halves(product(block, spread_ref[...], NT))
        both = product(jnp.concatenate(pooled, axis=0), block_ref[0, slot, 0, pixels:, :])
        sum_ref[...] += product(block, block_ref[0, slot, 0, :pixels, :]) + (both[:mid] + both[mid:])

    for slot in range(slots):
        block = target_ref[...]
        for i, (step, part) in enumerate(zip(steps, arrived)):
            if i in SPLIT_BLOCKS:
                came = joined(part[0], others[SPLIT_BLOCKS.index(i)][...])
            else:
                came = jnp.concatenate([part[0], part[1]], axis=1)
            block = jnp.where(held[slot] == step, came, block)
        held_ref[slot] = block
        pl.when(jnp.logical_and(active[slot], same))(lambda: add(slot, grad_ref))
        pl.when(jnp.logical_and(active[slot], jnp.logical_not(same)))(lambda: add(slot, other_ref))

    total = own_ref[...].astype(F32)
    nothing = jnp.zeros((mid, pixels // 2), BF16)
    for i, part in enumerate(arrived):
        last = part.shape[0] - 1
        if i in SPLIT_TERMS:
            came = joined(part[last], nothing)
        else:
            came = jnp.concatenate([part[last - 1], part[last]], axis=1)
        total = total + came.astype(F32)
    parts = jnp.concatenate(halves(jnp.concatenate([sum_ref[...], total], axis=1)), axis=0)
    weights = jnp.concatenate([proj_ref[...], proj_ref[...]], axis=0)
    out_ref[...] = product(weights, parts, TN) * factor
    parts, share, width = kept_ref.shape
    place = lax.axis_index("band")
    for k in range(band):
        first = pl.multiple_of(jnp.bitwise_xor(place, k) * share, share)
        for part in range(parts):
            out = out_ref[pl.ds(first, share), part * width : (part + 1) * width]
            if k == 0:
                kept_ref[part] = out
            else:
                sent_refs[k - 1][part] = out.astype(BF16)


def total_kernel(kept_ref, *refs):
    received, out_refs = refs[:-2], refs[-2:]
    rows = out_refs[0].shape[0]
    for i, out_ref in enumerate(out_refs):
        total = kept_ref[i * rows : (i + 1) * rows]
        for part in received:
            total = total + part[i * rows : (i + 1) * rows].astype(F32)
        out_ref[...] = total


def pyramid_kernel(
    band, factor, start_ref, count_ref, held_ref, other_ref, source_ref, proj_ref, spread_ref, pyramid_ref, scaled_ref
):
    mid = source_ref.shape[0]
    slot = pl.program_id(0)
    active = slot * band + lax.axis_index("band") < count_ref[0]
    same = lax.rem(start_ref[0] + 2 * BAND_REACH, 2) == 0

    @pl.when(slot == 0)
    def _():
        gram = product(proj_ref[...], proj_ref[...], NT)
        both = product(jnp.concatenate(halves(gram), axis=0), source_ref[...])
        high, low = halves((both[:mid] + both[mid:]) * factor)
        scaled_ref[:mid, :] = high
        scaled_ref[mid : 2 * mid, :] = low
        scaled_ref[2 * mid :, :] = high

    @pl.when(active)
    def _():
        target = jnp.where(same, held_ref[0], other_ref[0])
        pixels = target.shape[1]
        finest = product(jnp.concatenate([target, target], axis=0), scaled_ref[: 2 * mid, :], TN)
        pyramid_ref[0, 0, 0, :pixels, :] = finest.astype(BF16)
        high, low = halves(product(spread_ref[...], target, NT))
        coarser = product(jnp.concatenate([high, high, low], axis=1), scaled_ref[...])
        pyramid_ref[0, 0, 0, pixels:, :] = coarser.astype(BF16)

    @pl.when(jnp.logical_not(active))
    def _():
        pyramid_ref[0, 0, 0] = jnp.zeros(pyramid_ref.shape[3:], BF16)


def shards(frames, conv_weight, proj_weight, band_start, band_count, pyramid_grad):
    band = lax.axis_size("band")
    row_blocks = lax.axis_size("rows")
    mid, channels = proj_weight.shape
    share = channels // band
    factor = 1.0 / math.sqrt(channels)
    frames = jnp.swapaxes(frames, 2, 3)
    grad = jnp.swapaxes(pyramid_grad, 3, 4)
    slots = grad.shape[1]
    entries, pixels = grad.shape[3:]
    columns = frames.shape[3]
    half = columns // 2
    params = pltpu.CompilerParams(vmem_limit_bytes=VMEM_LIMIT)
    smem = pl.BlockSpec(memory_space=pltpu.SMEM)
    vmem = pl.BlockSpec(memory_space=pltpu.VMEM)
    spread = jnp.asarray(spread_matrix(pixels))

    table = step_table(band)
    steps = len(table[0])

    def along_rows(x, step):
        pairs = []
        for p in range(band):
            distance, turn = table[p][step]
            for row in range(row_blocks - distance):
                if row // distance % 2 == turn:
                    pairs.append((row * band + p, (row + distance) * band + p))
                    pairs.append(((row + distance) * band + p, row * band + p))
        return lax.ppermute(x, ("rows", "band"), pairs)

    def across(x, k):
        return lax.ppermute(x, "band", [(p, p ^ k) for p in range(band)])

    rim = lax.ppermute(frames[:, -1:], "rows", [(i, i + 1) for i in range(row_blocks - 1)])
    other_grad = across(grad, 1)
    picker = pl.pallas_call(
        picker_kernel,
        out_shape=jax.ShapeDtypeStruct((columns, 3 * half), BF16),
        compiler_params=params,
        cost_estimate=pl.CostEstimate(flops=2**33, bytes_accessed=2**21, transcendentals=0),
    )()
    lower, partial = pl.pallas_call(
        local_rows_kernel,
        out_shape=(
            jax.ShapeDtypeStruct((mid, columns), BF16),
            jax.ShapeDtypeStruct((mid, columns), F32),
        ),
        scratch_shapes=[pltpu.VMEM(frames.shape[:3] + (3 * half,), BF16)],
        compiler_params=params,
        cost_estimate=pl.CostEstimate(flops=2**31, bytes_accessed=2**21, transcendentals=0),
    )(picker, frames, conv_weight)

    block = jax.ShapeDtypeStruct((mid, pixels), BF16)
    piece = (mid, pixels // 2)
    split_terms = jax.ShapeDtypeStruct((len(SPLIT_TERMS), 2) + piece, BF16)
    messages = [
        jax.ShapeDtypeStruct(((1 if i in SPLIT_BLOCKS else 0) + 2,) + piece, BF16)
        for i in range(steps)
        if i not in SPLIT_TERMS
    ]
    target, source, own_term, terms, *messages = pl.pallas_call(
        lambda *refs: target_kernel(band, table, factor, *refs),
        in_specs=[smem] * 2 + [vmem] * 8,
        out_shape=(block, block, block, split_terms, *messages),
        scratch_shapes=[pltpu.VMEM((slots, mid, pixels), BF16)],
        compiler_params=params,
        cost_estimate=pl.CostEstimate(flops=2**31, bytes_accessed=2**22, transcendentals=0),
    )(band_start, band_count, rim, conv_weight, lower, partial, picker, grad, other_grad, spread)

    first = lax.axis_index("band") // 2 == 0
    others = across(jnp.where(first, terms[:, 1], terms[:, 0]), 2)
    terms = jnp.where(first, terms[:, 0], terms[:, 1])
    pieces = pl.pallas_call(
        pieces_kernel,
        out_shape=jax.ShapeDtypeStruct((2,) + piece, BF16),
        compiler_params=params,
        cost_estimate=pl.CostEstimate(flops=2**31, bytes_accessed=2**20, transcendentals=0),
    )(target)
    for i in range(len(messages)):
        if i not in SPLIT_BLOCKS:
            messages[i] = jnp.concatenate([pieces, messages[i]])
    for j, i in enumerate(SPLIT_TERMS):
        messages.insert(i, jnp.concatenate([pieces, terms[j : j + 1] + others[j : j + 1]]))
    arrived = [along_rows(messages[i], i) for i in range(steps)]
    other_blocks = [across(arrived[i][0], 2) for i in SPLIT_BLOCKS]

    out_parts = 2 * pixels // half
    part = (out_parts, share, half)
    held, kept, *sent = pl.pallas_call(
        lambda *refs: gradient_kernel(band, table, factor, *refs),
        in_specs=[smem] * 2 + [vmem] * (6 + steps + len(SPLIT_BLOCKS)),
        out_shape=(jax.ShapeDtypeStruct((slots, mid, pixels), BF16), jax.ShapeDtypeStruct(part, F32))
        + (jax.ShapeDtypeStruct(part, BF16),) * (band - 1),
        scratch_shapes=[pltpu.VMEM((mid, pixels), F32), pltpu.VMEM((channels, 2 * pixels), F32)],
        compiler_params=params,
        cost_estimate=pl.CostEstimate(flops=2**31, bytes_accessed=2**22, transcendentals=0),
    )(band_start, band_count, grad, other_grad, spread, proj_weight, target, own_term, *arrived, *other_blocks)

    received = [across(sent[k - 1], k) for k in reversed(range(1, band))]
    other = across(held, 1)

    def whole(shape):
        return pl.BlockSpec(shape, lambda j: (0,) * len(shape))

    target_spec = pl.BlockSpec((1, mid, pixels), lambda j: (j, 0, 0))
    grad_spec = pl.BlockSpec((1, 1, 1, entries, pixels), lambda j: (0, j, 0, 0, 0))
    pyramid = pl.pallas_call(
        lambda *refs: pyramid_kernel(band, factor, *refs),
        grid=(slots,),
        in_specs=[smem, smem, target_spec, target_spec, whole((mid, pixels)), whole((mid, channels))]
        + [whole(spread.shape)],
        out_specs=grad_spec,
        out_shape=jax.ShapeDtypeStruct(grad.shape, BF16),
        scratch_shapes=[pltpu.VMEM((3 * mid, pixels), BF16)],
        compiler_params=params,
        cost_estimate=pl.CostEstimate(flops=2**31, bytes_accessed=2**22, transcendentals=0),
    )(band_start, band_count, held, other, source, proj_weight, spread)

    kept, pyramid = lax.optimization_barrier((kept, pyramid))
    half_part = jax.ShapeDtypeStruct((out_parts // 2, share, half), F32)
    source_grad, target_grad = pl.pallas_call(
        total_kernel,
        out_shape=(half_part, half_part),
        compiler_params=params,
    )(kept, *received)
    return (jnp.swapaxes(pyramid, 3, 4), jnp.swapaxes(source_grad, 1, 2), jnp.swapaxes(target_grad, 1, 2))


def solution(mesh):
    in_specs = (
        P(None, "rows", None, None),
        P(),
        P(),
        P("rows"),
        P("rows"),
        P("rows", None, "band", None, None),
    )
    out_specs = (
        P("rows", None, "band", None, None),
        P("rows", None, "band"),
        P("rows", None, "band"),
    )
    return jax.shard_map(shards, mesh=mesh, in_specs=in_specs, out_specs=out_specs, check_vma=False)
```
